128 devices in a mesh: row: 8 (over x, core), mat: 16 (over z, y).
Axes of the slice: x: 4, y: 4, z: 4, core: 2. Of those that a mesh axis runs over, the one named last changes fastest.
Arguments:
- gradients: bfloat16 [4, 28672, 8192], P(None, 'row', 'mat'), may hold values from -140 to 140
- sketch: bfloat16 [8192, 256], P('mat'), may hold values from -0.0625 to 0.0625
Outputs:
- basis: bfloat16 [4, 28672, 256], P(None, ('row', 'mat'))
- projected: float32 [4, 256, 8192], P(None, 'row', 'mat')
The draws below stay inside these ranges and needn't reach their ends.
All inputs are finite; a program needn't handle non-finite values.
Results may differ from the reference program's by a relative error of at most 0.015.
Values may be sent and summed in bfloat16 or wider, within the bound.
No kernel may reach another device: no remote copies, remote signals or barrier semaphores. Data moves between devices by JAX's collectives and lax.ppermute only.
A program may use at most 128 MiB of HBM per device.

```python
import math
import jax
import jax.numpy as jnp
from jax import lax

ROWS = 28672
COLS = 8192
RANK = 256
MATS = 4


def draw_gradients(key, part):
    key = jax.random.fold_in(key, 11)
    base_key, row_key, col_key = jax.random.split(key, 3)
    shape = (MATS, ROWS, COLS)
    base = jnp.clip(jax.random.normal(base_key, shape, jnp.float32), -4.0, 4.0)
    spread = math.log(10.0)
    row_scale = jnp.exp(jax.random.uniform(row_key, (MATS, ROWS, 1), jnp.float32) * spread)
    position = jnp.arange(ROWS, dtype=jnp.float32).reshape(1, ROWS, 1) / ROWS
    row_scale = row_scale * jnp.exp(position * math.log(3.0))
    col_scale = jnp.exp(jax.random.uniform(col_key, (MATS, 1, COLS), jnp.float32) * spread)
    return (base * row_scale * col_scale * 0.1).astype(jnp.bfloat16)


def steps_of(key, shape, cuts, least, high):
    def one(dim, parts):
        heights = jax.random.uniform(jax.random.fold_in(jax.random.fold_in(key, 6), dim), (parts,), jnp.float32, least / len(cuts), high / len(cuts))
        return jnp.repeat(jnp.exp(heights), shape[dim] // parts).reshape((-1,) + (1,) * (len(shape) - dim - 1))

    level = one(*cuts[0])
    for cut in cuts[1:]:
        level = level * one(*cut)
    return level


def gaussian(own_key, dims, width, limit, pieces=(), kind=jnp.bfloat16):
    result = jax.random.normal(own_key, dims, jnp.float32) * width
    if len(pieces) > 0:
        result = steps_of(own_key, dims, pieces, -0.22, 0.18) * result
    return jnp.clip(result, min=-limit, max=limit).astype(kind)


def setup_inputs(seed: int = 0) -> dict:
    seeds = jax.random.split(jax.random.key(seed), 3)
    return {
        "gradients": draw_gradients(jax.random.fold_in(seeds[2], 71), 0),
        "sketch": gaussian(seeds[1], (COLS, RANK), COLS ** -0.5, 0.0625, ((0, 16),)),
    }


def reference(gradients, sketch):
    root = float(ROWS) ** 0.5
    bases = []
    projections = []
    for index in range(MATS):
        matrix = gradients[index]
        sketched = jnp.dot(matrix.astype(jnp.float32), sketch.astype(jnp.float32), preferred_element_type=jnp.float32)
        gram = jnp.dot(sketched.T.astype(jnp.float32), sketched.astype(jnp.float32), precision=lax.Precision.HIGHEST, preferred_element_type=jnp.float32)
        lower = jnp.linalg.cholesky(gram)
        qmat_t = lax.linalg.triangular_solve(lower, sketched.T, left_side=True, lower=True)
        basis = (qmat_t.T * root).astype(jnp.bfloat16)
        projected = jnp.dot(basis.T.astype(jnp.float32), matrix.astype(jnp.float32), preferred_element_type=jnp.float32) / root
        bases.append(basis)
        projections.append(projected)
    return (jnp.stack(bases), jnp.stack(projections))
```

```python
import functools

import jax
import jax.numpy as jnp
from jax import lax
from jax.experimental import pallas as pl
from jax.experimental.pallas import tpu as pltpu
from jax.sharding import PartitionSpec as P

MATS, RANK, SHARE, WIDTH, SHARES, RING = 4, 256, 224, 512, 16, 4
HALF = RANK // 2
BLOCK = RANK // 8
OFFS = (0, 1, 3, 2)
F32, BF16 = jnp.float32, jnp.bfloat16
EXACT = lax.Precision.HIGHEST
NEWTON_TOL = 1e-4
NEWTON_MAX = 10


def params():
    return pltpu.CompilerParams(vmem_limit_bytes=52 * 1024 * 1024)


def shift(value, axis, step):
    pairs = []
    if axis in ("y", "z"):
        for z in range(RING):
            for y in range(RING):
                to = z * RING + (y + step) % RING if axis == "y" else (z + step) % RING * RING + y
                pairs.append((z * RING + y, to))
        return lax.ppermute(value, "mat", pairs)
    for x in range(RING):
        for core in range(2):
            to = (x + step) % RING * 2 + core if axis == "x" else x * 2 + (core + step) % 2
            pairs.append((x * 2 + core, to))
    return lax.ppermute(value, "row", pairs)


def place():
    row, mat = lax.axis_index("row"), lax.axis_index("mat")
    return row // 2, row % 2, mat % RING, mat // RING


def chunk_row(index, along, dest):
    _, _, y, z = place()
    if along == "y":
        shares = [(z + off) % RING * RING + dest % RING for off in OFFS]
    else:
        shares = [dest % RING * RING + (y + off) % RING for off in OFFS]
    return jnp.stack([jnp.asarray(v, jnp.int32) for v in [index] + shares])


def gradient_specs(step=lambda *ids: ids[0]):
    return [
        pl.BlockSpec(
            (1, 1, SHARE, WIDTH),
            lambda *a, j=j: (a[-1][step(*a[:-1]), 0], a[-1][step(*a[:-1]), 1 + j], 0, 0),
        )
        for j in range(RING)
    ]


def sketch_kernel(tab, g0, g1, g2, g3, sk, *rest):
    out = rest[-1]
    for j, g in enumerate((g0, g1, g2, g3)):
        term = jnp.dot(g[0, 0], sk[...], preferred_element_type=F32)
        for other in rest[:-1]:
            term = term + other[0, j].astype(F32)
        out[0, j] = term.astype(out.dtype)


def sketch_chunks(grads, sketch, rows, recv=None):
    count = len(rows)
    block = (1, RING, SHARE, RANK)
    extra = [] if recv is None else [recv]
    return pl.pallas_call(
        sketch_kernel,
        grid_spec=pltpu.PrefetchScalarGridSpec(
            num_scalar_prefetch=1,
            grid=(count,),
            in_specs=gradient_specs()
            + [pl.BlockSpec((WIDTH, RANK), lambda n, t: (0, 0))]
            + [pl.BlockSpec(block, lambda n, t: (0, 0, 0, 0)) for _ in extra],
            out_specs=pl.BlockSpec(block, lambda n, t: (n, 0, 0, 0)),
        ),
        out_shape=jax.ShapeDtypeStruct((count,) + block[1:], BF16),
        compiler_params=params(),
    )(jnp.stack(rows), grads, grads, grads, grads, sketch, *extra)


def own_kernel(tab, g0, g1, g2, g3, sk, comb0, comb1, near0, near1, own, ahead, behind, across):
    first = pl.program_id(0) == 0

    def run(comb, near):
        for j, (g, out) in enumerate(zip((g0, g1, g2, g3), (own, ahead, behind, across))):
            term = jnp.dot(g[0, 0], sk[...], preferred_element_type=F32)
            term = term + comb[0, j].astype(F32) + near[0, j].astype(F32)
            out[0] = term.astype(out.dtype)

    pl.when(first)(lambda: run(comb0, near0))
    pl.when(jnp.logical_not(first))(lambda: run(comb1, near1))


def own_chunks(grads, sketch, rows, combs, nears):
    block = (1, RING, SHARE, RANK)
    share = pl.BlockSpec((1, SHARE, RANK), lambda n, t: (n, 0, 0))
    return pl.pallas_call(
        own_kernel,
        grid_spec=pltpu.PrefetchScalarGridSpec(
            num_scalar_prefetch=1,
            grid=(2,),
            in_specs=gradient_specs()
            + [pl.BlockSpec((WIDTH, RANK), lambda n, t: (0, 0))]
            + [pl.BlockSpec(block, lambda n, t: (0, 0, 0, 0))] * 2
            + [pl.BlockSpec(block, lambda n, t: (1, 0, 0, 0))] * 2,
            out_specs=[share] * 4,
        ),
        out_shape=[jax.ShapeDtypeStruct((2, SHARE, RANK), F32)]
        + [jax.ShapeDtypeStruct((2, SHARE, RANK), BF16)] * 3,
        compiler_params=params(),
    )(jnp.stack(rows), grads, grads, grads, grads, sketch, *combs, *nears)


def total_kernel(own, a, b, c, total, rounded, gram):
    value = own[0] + a[0].astype(F32) + b[0].astype(F32) + c[0].astype(F32)
    total[0] = value
    rounded[0] = value.astype(BF16)
    gram[0] = lax.dot_general(
        value, value, (((0,), (0,)), ((), ())), precision=EXACT, preferred_element_type=F32
    )


def totals(own, parts):
    share = pl.BlockSpec((1, SHARE, RANK), lambda n: (n, 0, 0))
    return pl.pallas_call(
        total_kernel,
        grid=(2,),
        in_specs=[share] * 4,
        out_specs=[share, share, pl.BlockSpec((1, RANK, RANK), lambda n: (n, 0, 0))],
        out_shape=[
            jax.ShapeDtypeStruct((2, SHARE, RANK), F32),
            jax.ShapeDtypeStruct((2, SHARE, RANK), BF16),
            jax.ShapeDtypeStruct((2, RANK, RANK), F32),
        ],
        compiler_params=params(),
    )(own, *parts)


def accumulate(chunk, grads):
    total = None
    for j, g in enumerate(grads):
        term = lax.dot_general(
            chunk[0, j], g[0, 0], (((0,), (0,)), ((), ())), preferred_element_type=F32
        )
        total = term if total is None else total + term
    return total


def gather_kernel(tab, g0, g1, g2, g3, c0, c1, c2, out):
    step = pl.program_id(1)
    grads = (g0, g1, g2, g3)

    @pl.when(step == 0)
    def _():
        out[0] = accumulate(c0, grads)

    @pl.when(step == 1)
    def _():
        out[0] += accumulate(c1, grads)

    @pl.when(step == 2)
    def _():
        out[0] += accumulate(c2, grads)


def project_three(grads, rows, chunks):
    block = (1, RING, SHARE, RANK)
    return pl.pallas_call(
        gather_kernel,
        grid_spec=pltpu.PrefetchScalarGridSpec(
            num_scalar_prefetch=1,
            grid=(2, 3),
            in_specs=gradient_specs(lambda m, k: m * 3 + k)
            + [pl.BlockSpec(block, lambda m, k, t: (m, 0, 0, 0))] * 3,
            out_specs=pl.BlockSpec((1, RANK, WIDTH), lambda m, k, t: (m, 0, 0)),
        ),
        out_shape=jax.ShapeDtypeStruct((2, RANK, WIDTH), F32),
        compiler_params=params(),
    )(jnp.stack(rows), grads, grads, grads, grads, *chunks)


def last_kernel(ranks, tab, g0, g1, g2, g3, c0, c1, part, inv, mine, theirs, rows, whole):
    first = pl.program_id(0) == 0
    grads = (g0, g1, g2, g3)

    @pl.when(first)
    def _():
        whole[...] = part[0] + accumulate(c0, grads)

    @pl.when(jnp.logical_not(first))
    def _():
        whole[...] = part[0] + accumulate(c1, grads)

    for b in range(8):
        start = pl.multiple_of(ranks[b] * BLOCK, BLOCK)
        rows[b * BLOCK : (b + 1) * BLOCK] = inv[0, pl.ds(start, BLOCK), :]
    out = jnp.dot(rows[...], whole[...], precision=EXACT, preferred_element_type=F32)
    mine[0] = out[:HALF]
    theirs[0] = out[HALF:].astype(BF16)


def project_last(grads, rows, chunks, part, inverse, pair, ranks):
    block = (1, RING, SHARE, RANK)
    return pl.pallas_call(
        last_kernel,
        grid_spec=pltpu.PrefetchScalarGridSpec(
            num_scalar_prefetch=2,
            grid=(2,),
            in_specs=gradient_specs(lambda n, r: n)
            + [pl.BlockSpec(block, lambda n, r, t: (0, 0, 0, 0))] * 2
            + [pl.BlockSpec((1, RANK, WIDTH), lambda n, r, t: (n, 0, 0))]
            + [pl.BlockSpec((1, RANK, RANK), lambda n, r, t: (pair * 2 + n, 0, 0))],
            out_specs=[pl.BlockSpec((1, HALF, WIDTH), lambda n, r, t: (n, 0, 0))] * 2,
            scratch_shapes=[pltpu.VMEM((RANK, RANK), F32), pltpu.VMEM((RANK, WIDTH), F32)],
        ),
        out_shape=[
            jax.ShapeDtypeStruct((2, HALF, WIDTH), F32),
            jax.ShapeDtypeStruct((2, HALF, WIDTH), BF16),
        ],
        compiler_params=params(),
    )(ranks, jnp.stack(rows), grads, grads, grads, grads, *chunks, part, inverse)


def basis_kernel(root, s, inv, out):
    value = lax.dot_general(
        s[0], inv[0], (((1,), (1,)), ((), ())), precision=EXACT, preferred_element_type=F32
    )
    out[0] = (value * root).astype(BF16)


def make_basis(total, inverse, pair, root):
    share = pl.BlockSpec((1, SHARE, RANK), lambda n: (n, 0, 0))
    return pl.pallas_call(
        functools.partial(basis_kernel, root),
        grid=(2,),
        in_specs=[share, pl.BlockSpec((1, RANK, RANK), lambda n: (pair * 2 + n, 0, 0))],
        out_specs=share,
        out_shape=jax.ShapeDtypeStruct((2, SHARE, RANK), BF16),
        compiler_params=params(),
    )(total, inverse)


def inverse_kernel(where, own, other, out, gram, scaled):
    x, core = where[0], where[1]
    for j, off in enumerate(OFFS):
        q = lax.rem(x + off, RING)
        half = pl.multiple_of(lax.rem(q, 2) * HALF, HALF)
        gram[core * 2 + q // 2, pl.ds(half, HALF), :] = own[j]
        gram[(1 - core) * 2 + q // 2, pl.ds(half, HALF), :] = other[j]
    rows = lax.broadcasted_iota(jnp.int32, (RANK, RANK), 0)
    cols = lax.broadcasted_iota(jnp.int32, (RANK, RANK), 1)
    eye = (rows == cols).astype(F32)
    weight = jnp.where(rows > cols, 1.0, 0.5 * eye)

    def diagonal(a, axis):
        return jnp.sum(jnp.where(rows == cols, a, 0.0), axis=axis, keepdims=True)

    def residual(value, a, precision):
        if precision is None:
            value = value.astype(BF16)
            a = a.astype(BF16)
        half = jnp.dot(value, a, precision=precision, preferred_element_type=F32)
        if precision is None:
            half = half.astype(BF16)
        return (
            lax.dot_general(
                half, value, (((1,), (1,)), ((), ())), precision=precision, preferred_element_type=F32
            )
            - eye
        )

    for m in range(MATS):
        a = gram[m]
        scaled[m] = a * lax.rsqrt(diagonal(a, 1)) * lax.rsqrt(diagonal(a, 0))
    for m in range(MATS):
        out[m] = eye - weight * (scaled[m] - eye)
    for _ in range(2):
        for m in range(MATS):
            value = out[m]
            error = (weight * residual(value, scaled[m], None)).astype(BF16)
            out[m] = value - jnp.dot(error, value.astype(BF16), preferred_element_type=F32)

    def exact_step(carry):
        count, _ = carry
        large = jnp.zeros((RANK, RANK), F32)
        for m in range(MATS):
            value = out[m]
            error = residual(value, scaled[m], EXACT)
            large = jnp.maximum(large, jnp.where(error == error, jnp.abs(error), 1e9))
            large = jnp.maximum(large, jnp.where((rows == cols) & (value <= 0.0), 1e9, 0.0))
            out[m] = value - jnp.dot(weight * error, value, precision=EXACT, preferred_element_type=F32)
        return count + 1, jnp.max(large)

    _, left = lax.while_loop(
        lambda c: (c[0] < NEWTON_MAX) & (c[1] > NEWTON_TOL) & (c[1] < 1e8),
        exact_step,
        (jnp.int32(0), jnp.float32(1.0)),
    )
    done = left <= NEWTON_TOL

    @pl.when(done)
    def _():
        for m in range(MATS):
            out[m] = out[m] * lax.rsqrt(diagonal(gram[m], 0))

    @pl.when(jnp.logical_not(done))
    def _():
        row_ids = lax.broadcasted_iota(jnp.int32, (RANK, 1), 0)
        col_ids = lax.broadcasted_iota(jnp.int32, (1, RANK), 1)

        def matrix(m, _):
            out[m] = eye

            def column(j, _):
                pivot_row = gram[m, pl.ds(j, 1), :]
                pivot = jnp.sum(jnp.where(col_ids == j, pivot_row, 0.0), axis=1, keepdims=True)
                values = jnp.sum(jnp.where(cols == j, gram[m], 0.0), axis=1, keepdims=True)
                factor = jnp.where(row_ids > j, values / pivot, 0.0)
                known = out[m, pl.ds(j, 1), :]
                gram[m] = gram[m] - factor * pivot_row
                out[m] = out[m] - factor * known
                out[m, pl.ds(j, 1), :] = known / jnp.sqrt(pivot)
                return 0

            return lax.fori_loop(0, RANK, column, 0)

        lax.fori_loop(0, MATS, matrix, 0)


def inverse_factors(where, own, other):
    return pl.pallas_call(
        inverse_kernel,
        grid_spec=pltpu.PrefetchScalarGridSpec(
            num_scalar_prefetch=1,
            grid=(1,),
            in_specs=[pl.BlockSpec((RING, HALF, RANK), lambda n, w: (0, 0, 0))] * 2,
            out_specs=pl.BlockSpec((MATS, RANK, RANK), lambda n, w: (0, 0, 0)),
            scratch_shapes=[
                pltpu.VMEM((MATS, RANK, RANK), F32),
                pltpu.VMEM((MATS, RANK, RANK), F32),
            ],
        ),
        out_shape=jax.ShapeDtypeStruct((MATS, RANK, RANK), F32),
        compiler_params=params(),
    )(where, own, other)


def from_others(value, axis):
    return [shift(value, axis, -1), shift(value, axis, 1), shift(value, axis, 2)]


def sum_and_factor(gram01, gram23):
    x, core, _, _ = place()
    first = core == 0
    keep = jnp.where(first, gram01, gram23)
    send = jnp.where(first, gram23, gram01)
    pair = (keep + shift(send, "core", 1)).reshape(RING, HALF, RANK)

    def piece(off):
        return lax.dynamic_index_in_dim(pair, (x + off) % RING, 0, keepdims=False)

    arrived = [shift(piece(1), "x", 1), shift(piece(3), "x", -1), shift(piece(2), "x", 2)]
    part = piece(0) + arrived[0] + arrived[1] + arrived[2]
    for axis in ("y", "z"):
        a, b, c = from_others(part, axis)
        part = part + a + b + c
    own = jnp.stack([part] + from_others(part, "x"))
    other = shift(own, "core", 1)
    return inverse_factors(jnp.stack([x, core]).astype(jnp.int32), own, other)


def local(gradients, sketch):
    root = float(gradients.shape[1] * lax.axis_size("row")) ** 0.5
    grads = gradients.reshape(MATS, SHARES, SHARE, WIDTH)
    x, core, y, z = place()
    here = {"y": y, "z": z}
    pairs = (("y", "z"), ("z", "y"))

    hop1 = {}
    for sign in (1, -1):
        for p, (ring, _) in enumerate(pairs):
            far, near = (2 * p, 2 * p + 1) if sign == 1 else (2 * p + 1, 2 * p)
            rows = [
                chunk_row(far, ring, here[ring] + 2),
                chunk_row(near, ring, here[ring] + (sign % RING)),
            ]
            hop1[p, sign] = shift(sketch_chunks(grads, sketch, rows), ring, sign)
    hop2 = {}
    for sign in (1, -1):
        for p, (ring, _) in enumerate(pairs):
            far = 2 * p if sign == 1 else 2 * p + 1
            rows = [chunk_row(far, ring, here[ring] + (sign % RING))]
            hop2[p, sign] = shift(sketch_chunks(grads, sketch, rows, hop1[p, sign]), ring, sign)
    total, rounded, gram = [], [], []
    for p, (ring, cross) in enumerate(pairs):
        rows = [chunk_row(2 * p + i, ring, here[ring]) for i in range(2)]
        own, ahead, behind, across = own_chunks(
            grads, sketch, rows, (hop2[p, 1], hop2[p, -1]), (hop1[p, -1], hop1[p, 1])
        )
        parts = [shift(ahead, cross, 1), shift(behind, cross, -1), shift(across, cross, 2)]
        outs = totals(own, parts)
        for store, value in zip((total, rounded, gram), outs):
            store.append(value)

    inverse = sum_and_factor(*gram)

    ranks = [(x + off) % RING * 2 + core for off in OFFS]
    ranks += [(x + off) % RING * 2 + 1 - core for off in OFFS]
    ranks = jnp.stack(ranks).astype(jnp.int32)
    chunks, nexts, backs, befores, afters = [], [], [], [], []
    for p, (ring, cross) in enumerate(pairs):
        chunks.append(jnp.stack([rounded[p]] + from_others(rounded[p], cross), axis=1))
    for p, (ring, _) in enumerate(pairs):
        befores.append(shift(chunks[p], ring, 1))
        afters.append(shift(chunks[p], ring, -1))
    for p, (ring, _) in enumerate(pairs):
        nexts.append(shift(befores[p][0:1], ring, 1))
        backs.append(shift(afters[p][1:2], ring, -1))
    mine, theirs, basis = [], [], []
    for p, (ring, _) in enumerate(pairs):
        rows = [chunk_row(2 * p + i, ring, here[ring] + off) for i in range(2) for off in (0, 3, 1)]
        part = project_three(grads, rows, (chunks[p], befores[p], afters[p]))
        rows = [chunk_row(2 * p + i, ring, here[ring] + 2) for i in range(2)]
        a, b = project_last(grads, rows, (nexts[p], backs[p]), part, inverse, p, ranks)
        mine.append(a.reshape(2, RING, BLOCK, WIDTH))
        theirs.append(shift(b, "core", 1).reshape(2, RING, BLOCK, WIDTH))
        basis.append(make_basis(total[p], inverse, p, root))
    both = jnp.concatenate(
        [m + t.astype(F32) for m, t in zip(mine, theirs)], axis=0
    )
    out = both[:, 0]
    for j, step in ((1, 1), (2, -1), (3, 2)):
        out = out + shift(both[:, j].astype(BF16), "x", step).astype(F32)
    return jnp.concatenate(basis, axis=0), out


def solution(mesh):
    placed = (P(None, "row", "mat"), P("mat", None))
    return jax.shard_map(
        local,
        mesh=mesh,
        in_specs=placed,
        out_specs=(P(None, ("row", "mat"), None), P(None, "row", "mat")),
        check_vma=False,
    )
```

```python
import functools

import jax
import jax.numpy as jnp
from jax import lax
from jax.experimental import pallas as pl
from jax.experimental.pallas import tpu as pltpu
from jax.sharding import PartitionSpec as P

MATS, RANK, SHARE, WIDTH, SHARES, RING = 4, 256, 224, 512, 16, 4
HALF = RANK // 2
BLOCK = RANK // 8
OFFS = (0, 1, 3, 2)
F32, BF16 = jnp.float32, jnp.bfloat16
EXACT = lax.Precision.HIGHEST
NEWTON_TOL = 1e-4
NEWTON_MAX = 10


def params():
    return pltpu.CompilerParams(vmem_limit_bytes=52 * 1024 * 1024)


def cost(flops, moved):
    return pl.CostEstimate(flops=int(flops), bytes_accessed=int(moved), transcendentals=0)


def shift(value, axis, step):
    pairs = []
    if axis in ("y", "z"):
        for z in range(RING):
            for y in range(RING):
                to = z * RING + (y + step) % RING if axis == "y" else (z + step) % RING * RING + y
                pairs.append((z * RING + y, to))
        return lax.ppermute(value, "mat", pairs)
    for x in range(RING):
        for core in range(2):
            to = (x + step) % RING * 2 + core if axis == "x" else x * 2 + (core + step) % 2
            pairs.append((x * 2 + core, to))
    return lax.ppermute(value, "row", pairs)


def place():
    row, mat = lax.axis_index("row"), lax.axis_index("mat")
    return row // 2, row % 2, mat % RING, mat // RING


def chunk_row(index, along, dest):
    _, _, y, z = place()
    if along == "y":
        shares = [(z + off) % RING * RING + dest % RING for off in OFFS]
    else:
        shares = [dest % RING * RING + (y + off) % RING for off in OFFS]
    return jnp.stack([jnp.asarray(v, jnp.int32) for v in [index] + shares])


def gradient_specs(step=lambda *ids: ids[0]):
    return [
        pl.BlockSpec(
            (1, 1, SHARE, WIDTH),
            lambda *a, j=j: (a[-1][step(*a[:-1]), 0], a[-1][step(*a[:-1]), 1 + j], 0, 0),
        )
        for j in range(RING)
    ]


def sketch_of(grads, sk):
    rows = jnp.concatenate([g[0, 0] for g in grads], axis=0)
    return jnp.dot(rows, sk[...], preferred_element_type=F32)


CHUNK = RING * SHARE
CHUNK_FLOPS = 2 * CHUNK * WIDTH * RANK
CHUNK_BYTES = 2 * CHUNK * (WIDTH + 2 * RANK)
CHUNK_BLOCK = (1, CHUNK, RANK)


def sketch_kernel(tab, g0, g1, g2, g3, sk, out0, out1):
    def run(out):
        out[0] = sketch_of((g0, g1, g2, g3), sk).astype(BF16)

    pl.when(pl.program_id(0) < 2)(lambda: run(out0))
    pl.when(pl.program_id(0) >= 2)(lambda: run(out1))


def sketch_chunks(grads, sketch, rows):
    return pl.pallas_call(
        sketch_kernel,
        grid_spec=pltpu.PrefetchScalarGridSpec(
            num_scalar_prefetch=1,
            grid=(4,),
            in_specs=gradient_specs() + [pl.BlockSpec((WIDTH, RANK), lambda n, t: (0, 0))],
            out_specs=[
                pl.BlockSpec(CHUNK_BLOCK, lambda n, t: (jnp.minimum(n, 1), 0, 0)),
                pl.BlockSpec(CHUNK_BLOCK, lambda n, t: (jnp.maximum(n - 2, 0), 0, 0)),
            ],
        ),
        out_shape=[jax.ShapeDtypeStruct((2, CHUNK, RANK), BF16)] * 2,
        compiler_params=params(),
        cost_estimate=cost(4 * CHUNK_FLOPS, 4 * CHUNK_BYTES),
    )(jnp.stack(rows), grads, grads, grads, grads, sketch)


def combine_kernel(tab, g0, g1, g2, g3, sk, recv0, recv1, out0, out1):
    def run(recv, out):
        term = sketch_of((g0, g1, g2, g3), sk)
        out[0] = (term + recv[0].astype(F32)).astype(BF16)

    pl.when(pl.program_id(0) == 0)(lambda: run(recv0, out0))
    pl.when(pl.program_id(0) == 1)(lambda: run(recv1, out1))


def combined_chunks(grads, sketch, rows, recvs):
    block = pl.BlockSpec(CHUNK_BLOCK, lambda n, t: (0, 0, 0))
    return pl.pallas_call(
        combine_kernel,
        grid_spec=pltpu.PrefetchScalarGridSpec(
            num_scalar_prefetch=1,
            grid=(2,),
            in_specs=gradient_specs()
            + [pl.BlockSpec((WIDTH, RANK), lambda n, t: (0, 0)), block, block],
            out_specs=[block, block],
        ),
        out_shape=[jax.ShapeDtypeStruct((1, CHUNK, RANK), BF16)] * 2,
        compiler_params=params(),
        cost_estimate=cost(2 * CHUNK_FLOPS, 2 * CHUNK_BYTES),
    )(jnp.stack(rows), grads, grads, grads, grads, sketch, *recvs)


def own_kernel(tab, g0, g1, g2, g3, sk, comb0, comb1, near0, near1, own, ahead, behind, across):
    def run(comb, near):
        term = sketch_of((g0, g1, g2, g3), sk)
        term = term + comb[0].astype(F32) + near[0].astype(F32)
        for j, out in enumerate((own, ahead, behind, across)):
            out[0] = term[j * SHARE : (j + 1) * SHARE].astype(out.dtype)

    pl.when(pl.program_id(0) == 0)(lambda: run(comb0, near0))
    pl.when(pl.program_id(0) == 1)(lambda: run(comb1, near1))


def own_chunks(grads, sketch, rows, combs, nears):
    share = pl.BlockSpec((1, SHARE, RANK), lambda n, t: (n, 0, 0))
    return pl.pallas_call(
        own_kernel,
        grid_spec=pltpu.PrefetchScalarGridSpec(
            num_scalar_prefetch=1,
            grid=(2,),
            in_specs=gradient_specs()
            + [pl.BlockSpec((WIDTH, RANK), lambda n, t: (0, 0))]
            + [pl.BlockSpec(CHUNK_BLOCK, lambda n, t: (0, 0, 0))] * 2
            + [pl.BlockSpec(CHUNK_BLOCK, lambda n, t: (1, 0, 0))] * 2,
            out_specs=[share] * 4,
        ),
        out_shape=[jax.ShapeDtypeStruct((2, SHARE, RANK), F32)]
        + [jax.ShapeDtypeStruct((2, SHARE, RANK), BF16)] * 3,
        compiler_params=params(),
        cost_estimate=cost(2 * CHUNK_FLOPS, 2 * CHUNK_BYTES),
    )(jnp.stack(rows), grads, grads, grads, grads, sketch, *combs, *nears)


def total_kernel(own, a, b, c, total, rounded, gram):
    value = own[0] + a[0].astype(F32) + b[0].astype(F32) + c[0].astype(F32)
    total[0] = value
    rounded[0] = value.astype(BF16)
    gram[0] = lax.dot_general(
        value, value, (((0,), (0,)), ((), ())), precision=EXACT, preferred_element_type=F32
    )


def totals(own, parts):
    share = pl.BlockSpec((1, SHARE, RANK), lambda n: (n, 0, 0))
    return pl.pallas_call(
        total_kernel,
        grid=(2,),
        in_specs=[share] * 4,
        out_specs=[share, share, pl.BlockSpec((1, RANK, RANK), lambda n: (n, 0, 0))],
        out_shape=[
            jax.ShapeDtypeStruct((2, SHARE, RANK), F32),
            jax.ShapeDtypeStruct((2, SHARE, RANK), BF16),
            jax.ShapeDtypeStruct((2, RANK, RANK), F32),
        ],
        compiler_params=params(),
        cost_estimate=cost(2 * 12 * SHARE * RANK * RANK, 2 * SHARE * RANK * 16),
    )(own, *parts)


def project_kernel(ranks, s, g, inv, mine, theirs, rows):
    whole = lax.dot_general(
        s[0], g[0], (((0,), (0,)), ((), ())), preferred_element_type=F32
    )
    for b in range(8):
        start = pl.multiple_of(ranks[b] * BLOCK, BLOCK)
        rows[b * BLOCK : (b + 1) * BLOCK] = inv[0, pl.ds(start, BLOCK), :]
    out = jnp.dot(rows[...], whole, precision=EXACT, preferred_element_type=F32)
    mine[0] = out[:HALF]
    theirs[0] = out[HALF:].astype(BF16)


def project(gradients, gathered, inverse, ranks):
    depth = gradients.shape[1]
    half = pl.BlockSpec((1, HALF, WIDTH), lambda n, r: (n, 0, 0))
    return pl.pallas_call(
        project_kernel,
        grid_spec=pltpu.PrefetchScalarGridSpec(
            num_scalar_prefetch=1,
            grid=(MATS,),
            in_specs=[
                pl.BlockSpec((1, depth, RANK), lambda n, r: (n, 0, 0)),
                pl.BlockSpec((1, depth, WIDTH), lambda n, r: (n, 0, 0)),
                pl.BlockSpec((1, RANK, RANK), lambda n, r: (n, 0, 0)),
            ],
            out_specs=[half, half],
            scratch_shapes=[pltpu.VMEM((RANK, RANK), F32)],
        ),
        out_shape=[
            jax.ShapeDtypeStruct((MATS, HALF, WIDTH), F32),
            jax.ShapeDtypeStruct((MATS, HALF, WIDTH), BF16),
        ],
        compiler_params=params(),
        cost_estimate=cost(MATS * 2 * RANK * WIDTH * (depth + 6 * RANK), MATS * 2 * depth * (WIDTH + RANK)),
    )(ranks, gathered, gradients, inverse)


def basis_kernel(root, s, inv, out):
    value = lax.dot_general(
        s[0], inv[0], (((1,), (1,)), ((), ())), precision=EXACT, preferred_element_type=F32
    )
    out[0] = (value * root).astype(BF16)


def make_basis(total, inverse, root):
    share = pl.BlockSpec((1, SHARE, RANK), lambda n: (n, 0, 0))
    return pl.pallas_call(
        functools.partial(basis_kernel, root),
        grid=(MATS,),
        in_specs=[share, pl.BlockSpec((1, RANK, RANK), lambda n: (n, 0, 0))],
        out_specs=share,
        out_shape=jax.ShapeDtypeStruct((MATS, SHARE, RANK), BF16),
        compiler_params=params(),
        cost_estimate=cost(4 * 12 * SHARE * RANK * RANK, 4 * SHARE * RANK * 10),
    )(total, inverse)


def inverse_kernel(where, own, other, out, gram, scaled):
    x, core = where[0], where[1]
    for j, off in enumerate(OFFS):
        q = lax.rem(x + off, RING)
        half = pl.multiple_of(lax.rem(q, 2) * HALF, HALF)
        gram[core * 2 + q // 2, pl.ds(half, HALF), :] = own[j]
        gram[(1 - core) * 2 + q // 2, pl.ds(half, HALF), :] = other[j]
    rows = lax.broadcasted_iota(jnp.int32, (RANK, RANK), 0)
    cols = lax.broadcasted_iota(jnp.int32, (RANK, RANK), 1)
    eye = (rows == cols).astype(F32)
    weight = jnp.where(rows > cols, 1.0, 0.5 * eye)

    def diagonal(a, axis):
        return jnp.sum(jnp.where(rows == cols, a, 0.0), axis=axis, keepdims=True)

    def residual(value, a, precision):
        if precision is None:
            value = value.astype(BF16)
            a = a.astype(BF16)
        half = jnp.dot(value, a, precision=precision, preferred_element_type=F32)
        if precision is None:
            half = half.astype(BF16)
        return (
            lax.dot_general(
                half, value, (((1,), (1,)), ((), ())), precision=precision, preferred_element_type=F32
            )
            - eye
        )

    for m in range(MATS):
        a = gram[m]
        scaled[m] = a * lax.rsqrt(diagonal(a, 1)) * lax.rsqrt(diagonal(a, 0))
    for m in range(MATS):
        out[m] = eye - weight * (scaled[m] - eye)
    for _ in range(2):
        for m in range(MATS):
            value = out[m]
            error = (weight * residual(value, scaled[m], None)).astype(BF16)
            out[m] = value - jnp.dot(error, value.astype(BF16), preferred_element_type=F32)

    def exact_step(carry):
        count, _ = carry
        large = jnp.zeros((RANK, RANK), F32)
        for m in range(MATS):
            value = out[m]
            error = residual(value, scaled[m], EXACT)
            large = jnp.maximum(large, jnp.where(error == error, jnp.abs(error), 1e9))
            large = jnp.maximum(large, jnp.where((rows == cols) & (value <= 0.0), 1e9, 0.0))
            out[m] = value - jnp.dot(weight * error, value, precision=EXACT, preferred_element_type=F32)
        return count + 1, jnp.max(large)

    _, left = lax.while_loop(
        lambda c: (c[0] < NEWTON_MAX) & (c[1] > NEWTON_TOL) & (c[1] < 1e8),
        exact_step,
        (jnp.int32(0), jnp.float32(1.0)),
    )
    done = left <= NEWTON_TOL

    @pl.when(done)
    def _():
        for m in range(MATS):
            out[m] = out[m] * lax.rsqrt(diagonal(gram[m], 0))

    @pl.when(jnp.logical_not(done))
    def _():
        row_ids = lax.broadcasted_iota(jnp.int32, (RANK, 1), 0)
        col_ids = lax.broadcasted_iota(jnp.int32, (1, RANK), 1)

        def matrix(m, _):
            out[m] = eye

            def column(j, _):
                pivot_row = gram[m, pl.ds(j, 1), :]
                pivot = jnp.sum(jnp.where(col_ids == j, pivot_row, 0.0), axis=1, keepdims=True)
                values = jnp.sum(jnp.where(cols == j, gram[m], 0.0), axis=1, keepdims=True)
                factor = jnp.where(row_ids > j, values / pivot, 0.0)
                known = out[m, pl.ds(j, 1), :]
                gram[m] = gram[m] - factor * pivot_row
                out[m] = out[m] - factor * known
                out[m, pl.ds(j, 1), :] = known / jnp.sqrt(pivot)
                return 0

            return lax.fori_loop(0, RANK, column, 0)

        lax.fori_loop(0, MATS, matrix, 0)


def inverse_factors(where, own, other):
    return pl.pallas_call(
        inverse_kernel,
        grid_spec=pltpu.PrefetchScalarGridSpec(
            num_scalar_prefetch=1,
            grid=(1,),
            in_specs=[pl.BlockSpec((RING, HALF, RANK), lambda n, w: (0, 0, 0))] * 2,
            out_specs=pl.BlockSpec((MATS, RANK, RANK), lambda n, w: (0, 0, 0)),
            scratch_shapes=[
                pltpu.VMEM((MATS, RANK, RANK), F32),
                pltpu.VMEM((MATS, RANK, RANK), F32),
            ],
        ),
        out_shape=jax.ShapeDtypeStruct((MATS, RANK, RANK), F32),
        compiler_params=params(),
        cost_estimate=cost(12e9, 4 * MATS * RANK * RANK * 4),
    )(where, own, other)


def from_others(value, axis):
    return [shift(value, axis, -1), shift(value, axis, 1), shift(value, axis, 2)]


def sum_and_factor(send, keep):
    x, core, _, _ = place()
    pair = (keep + shift(send, "core", 1)).reshape(RING, HALF, RANK)

    def piece(off):
        return lax.dynamic_index_in_dim(pair, (x + off) % RING, 0, keepdims=False)

    arrived = [shift(piece(1), "x", 1), shift(piece(3), "x", -1), shift(piece(2), "x", 2)]
    part = piece(0) + arrived[0] + arrived[1] + arrived[2]
    for axis in ("y", "z"):
        a, b, c = from_others(part, axis)
        part = part + a + b + c
    own = jnp.stack([part] + from_others(part, "x"))
    other = shift(own, "core", 1)
    return inverse_factors(jnp.stack([x, core]).astype(jnp.int32), own, other)


def local(gradients, sketch):
    root = float(gradients.shape[1] * lax.axis_size("row")) ** 0.5
    grads = gradients.reshape(MATS, SHARES, SHARE, WIDTH)
    x, core, y, z = place()
    here = {"y": y, "z": z}
    pairs = (("y", "z"), ("z", "y"))

    hop1 = {}
    for sign in (1, -1):
        rows = []
        for p, (ring, _) in enumerate(pairs):
            far, near = (2 * p, 2 * p + 1) if sign == 1 else (2 * p + 1, 2 * p)
            rows += [
                chunk_row(far, ring, here[ring] + 2),
                chunk_row(near, ring, here[ring] + (sign % RING)),
            ]
        for p, sent in enumerate(sketch_chunks(grads, sketch, rows)):
            hop1[p, sign] = shift(sent, pairs[p][0], sign)
    hop2 = {}
    for sign in (1, -1):
        rows = []
        for p, (ring, _) in enumerate(pairs):
            far = 2 * p if sign == 1 else 2 * p + 1
            rows.append(chunk_row(far, ring, here[ring] + (sign % RING)))
        sums = combined_chunks(grads, sketch, rows, (hop1[0, sign], hop1[1, sign]))
        for p, sent in enumerate(sums):
            hop2[p, sign] = shift(sent, pairs[p][0], sign)
    hop2 = dict(zip(hop2, lax.optimization_barrier(tuple(hop2.values()))))
    owns, parts = [], []
    for p, (ring, cross) in enumerate(pairs):
        rows = [chunk_row(2 * p + i, ring, here[ring]) for i in range(2)]
        own, ahead, behind, across = own_chunks(
            grads, sketch, rows, (hop2[p, 1], hop2[p, -1]), (hop1[p, -1], hop1[p, 1])
        )
        owns.append(own)
        parts.append([shift(ahead, cross, 1), shift(behind, cross, -1), shift(across, cross, 2)])
    total, rounded, gram = zip(*(totals(own, arrived) for own, arrived in zip(owns, parts)))
    send = jnp.where(core == 0, gram[1], gram[0])
    keep = jnp.where(core == 0, gram[0], gram[1])

    gathered = lax.all_gather(jnp.concatenate(rounded, axis=0), "mat", axis=1, tiled=True)
    inverse = sum_and_factor(send, keep)

    ranks = [(x + off) % RING * 2 + core for off in OFFS]
    ranks += [(x + off) % RING * 2 + 1 - core for off in OFFS]
    ranks = jnp.stack(ranks).astype(jnp.int32)
    basis = make_basis(jnp.concatenate(total, axis=0), inverse, root)
    mine, theirs = project(gradients, gathered, inverse, ranks)
    both = (mine + shift(theirs, "core", 1).astype(F32)).reshape(MATS, RING, BLOCK, WIDTH)
    out = both[:, 0]
    for j, step in ((1, 1), (2, -1), (3, 2)):
        out = out + shift(both[:, j].astype(BF16), "x", step).astype(F32)
    return basis, out


def solution(mesh):
    placed = (P(None, "row", "mat"), P("mat", None))
    return jax.shard_map(
        local,
        mesh=mesh,
        in_specs=placed,
        out_specs=(P(None, ("row", "mat"), None), P(None, "row", "mat")),
        check_vma=False,
    )
```

```python
import functools

import jax
import jax.numpy as jnp
from jax import lax
from jax.experimental import pallas as pl
from jax.experimental.pallas import tpu as pltpu
from jax.sharding import PartitionSpec as P

MATS, RANK, SHARE, WIDTH, SHARES, RING = 4, 256, 224, 512, 16, 4
HALF = RANK // 2
BLOCK = RANK // 8
OFFS = (0, 1, 3, 2)
F32, BF16 = jnp.float32, jnp.bfloat16
EXACT = lax.Precision.HIGHEST
NEWTON_TOL = 3e-4
NEWTON_MAX = 10


def params():
    return pltpu.CompilerParams(vmem_limit_bytes=52 * 1024 * 1024)


def cost(flops, moved):
    return pl.CostEstimate(flops=int(flops), bytes_accessed=int(moved), transcendentals=0)


def shift(value, axis, step):
    pairs = []
    if axis in ("y", "z"):
        for z in range(RING):
            for y in range(RING):
                to = z * RING + (y + step) % RING if axis == "y" else (z + step) % RING * RING + y
                pairs.append((z * RING + y, to))
        return lax.ppermute(value, "mat", pairs)
    for x in range(RING):
        for core in range(2):
            to = (x + step) % RING * 2 + core if axis == "x" else x * 2 + (core + step) % 2
            pairs.append((x * 2 + core, to))
    return lax.ppermute(value, "row", pairs)


def place():
    row, mat = lax.axis_index("row"), lax.axis_index("mat")
    return row // 2, row % 2, mat % RING, mat // RING


def chunk_row(index, along, dest):
    _, _, y, z = place()
    if along == "y":
        return [index] + [(z + off) % RING * RING + dest % RING for off in OFFS]
    return [index] + [dest % RING * RING + (y + off) % RING for off in OFFS]


def gradient_specs(base, step=lambda *ids: ids[0]):
    return [
        pl.BlockSpec(
            (1, 1, SHARE, WIDTH),
            lambda *a, j=j: (a[-1][base + step(*a[:-1]), 0], a[-1][base + step(*a[:-1]), 1 + j], 0, 0),
        )
        for j in range(RING)
    ]


def sketch_of(grads, sk):
    rows = jnp.concatenate([g[0, 0] for g in grads], axis=0)
    return jnp.dot(rows, sk[...], preferred_element_type=F32)


CHUNK = RING * SHARE
CHUNK_FLOPS = 2 * CHUNK * WIDTH * RANK
CHUNK_BYTES = 2 * CHUNK * (WIDTH + 2 * RANK)
CHUNK_BLOCK = (1, CHUNK, RANK)


def sketch_kernel(tab, g0, g1, g2, g3, sk, *outs):
    def run(out):
        out[0] = sketch_of((g0, g1, g2, g3), sk).astype(BF16)

    for n, out in enumerate(outs):
        pl.when(pl.program_id(0) == n)(lambda out=out: run(out))


def sketch_chunks(grads, sketch, table, base):
    return pl.pallas_call(
        sketch_kernel,
        grid_spec=pltpu.PrefetchScalarGridSpec(
            num_scalar_prefetch=1,
            grid=(4,),
            in_specs=gradient_specs(base) + [pl.BlockSpec((WIDTH, RANK), lambda n, t: (0, 0))],
            out_specs=[pl.BlockSpec(CHUNK_BLOCK, lambda n, t: (0, 0, 0))] * 4,
        ),
        out_shape=[jax.ShapeDtypeStruct((1, CHUNK, RANK), BF16)] * 4,
        compiler_params=params(),
        cost_estimate=cost(4 * CHUNK_FLOPS, 4 * CHUNK_BYTES),
    )(table, grads, grads, grads, grads, sketch)


def combine_kernel(tab, g0, g1, g2, g3, sk, recv0, recv1, out0, out1):
    def run(recv, out):
        term = sketch_of((g0, g1, g2, g3), sk)
        out[0] = (term + recv[0].astype(F32)).astype(BF16)

    pl.when(pl.program_id(0) == 0)(lambda: run(recv0, out0))
    pl.when(pl.program_id(0) == 1)(lambda: run(recv1, out1))


def combined_chunks(grads, sketch, table, base, recvs):
    block = pl.BlockSpec(CHUNK_BLOCK, lambda n, t: (0, 0, 0))
    return pl.pallas_call(
        combine_kernel,
        grid_spec=pltpu.PrefetchScalarGridSpec(
            num_scalar_prefetch=1,
            grid=(2,),
            in_specs=gradient_specs(base)
            + [pl.BlockSpec((WIDTH, RANK), lambda n, t: (0, 0)), block, block],
            out_specs=[block, block],
        ),
        out_shape=[jax.ShapeDtypeStruct((1, CHUNK, RANK), BF16)] * 2,
        compiler_params=params(),
        cost_estimate=cost(2 * CHUNK_FLOPS, 2 * CHUNK_BYTES),
    )(table, grads, grads, grads, grads, sketch, *recvs)


def near_kernel(tab, g0, g1, g2, g3, sk, near0, near1, out):
    def run(near):
        out[0] = sketch_of((g0, g1, g2, g3), sk) + near[0].astype(F32)

    pl.when(pl.program_id(0) == 0)(lambda: run(near0))
    pl.when(pl.program_id(0) == 1)(lambda: run(near1))


def own_and_near(grads, sketch, table, base, nears):
    return pl.pallas_call(
        near_kernel,
        grid_spec=pltpu.PrefetchScalarGridSpec(
            num_scalar_prefetch=1,
            grid=(2,),
            in_specs=gradient_specs(base)
            + [pl.BlockSpec((WIDTH, RANK), lambda n, t: (0, 0))]
            + [pl.BlockSpec(CHUNK_BLOCK, lambda n, t: (0, 0, 0))] * 2,
            out_specs=pl.BlockSpec(CHUNK_BLOCK, lambda n, t: (n, 0, 0)),
        ),
        out_shape=jax.ShapeDtypeStruct((2, CHUNK, RANK), F32),
        compiler_params=params(),
        cost_estimate=cost(2 * CHUNK_FLOPS, 2 * CHUNK_BYTES),
    )(table, grads, grads, grads, grads, sketch, *nears)


def own_kernel(part, comb0, comb1, own, ahead, behind, across):
    def run(comb):
        for j, out in enumerate((own, ahead, behind, across)):
            rows = slice(j * SHARE, (j + 1) * SHARE)
            out[0] = (part[0, rows] + comb[0, rows].astype(F32)).astype(out.dtype)

    pl.when(pl.program_id(0) == 0)(lambda: run(comb0))
    pl.when(pl.program_id(0) == 1)(lambda: run(comb1))


def own_chunks(part, combs):
    share = pl.BlockSpec((1, SHARE, RANK), lambda n: (n, 0, 0))
    return pl.pallas_call(
        own_kernel,
        grid=(2,),
        in_specs=[pl.BlockSpec(CHUNK_BLOCK, lambda n: (n, 0, 0))]
        + [pl.BlockSpec(CHUNK_BLOCK, lambda n: (0, 0, 0))] * 2,
        out_specs=[share] * 4,
        out_shape=[jax.ShapeDtypeStruct((2, SHARE, RANK), F32)]
        + [jax.ShapeDtypeStruct((2, SHARE, RANK), BF16)] * 3,
        compiler_params=params(),
        cost_estimate=cost(2 * CHUNK * RANK, 16 * CHUNK * RANK),
    )(part, *combs)


def total_kernel(own, a, b, c, total, rounded):
    value = own[0] + a[0].astype(F32) + b[0].astype(F32) + c[0].astype(F32)
    total[0] = value
    rounded[0] = value.astype(BF16)


def totals(own, parts):
    share = pl.BlockSpec((1, SHARE, RANK), lambda n: (n, 0, 0))
    return pl.pallas_call(
        total_kernel,
        grid=(2,),
        in_specs=[share] * 4,
        out_specs=[share, share],
        out_shape=[
            jax.ShapeDtypeStruct((2, SHARE, RANK), F32),
            jax.ShapeDtypeStruct((2, SHARE, RANK), BF16),
        ],
        compiler_params=params(),
        cost_estimate=cost(2 * SHARE * RANK, 2 * SHARE * RANK * 16),
    )(own, *parts)


TRI = 3


def gram_kernel(s, out):
    left = jnp.transpose(s[0])
    out[0, 0] = jnp.dot(left[:HALF], s[0, :, :HALF], precision=EXACT, preferred_element_type=F32)
    low = jnp.dot(left[HALF:], s[0], precision=EXACT, preferred_element_type=F32)
    out[0, 1] = low[:, :HALF]
    out[0, 2] = low[:, HALF:]


def gram_parts(total):
    return pl.pallas_call(
        gram_kernel,
        grid=(MATS,),
        in_specs=[pl.BlockSpec((1, SHARE, RANK), lambda n: (n, 0, 0))],
        out_specs=pl.BlockSpec((1, TRI, HALF, HALF), lambda n: (n, 0, 0, 0)),
        out_shape=jax.ShapeDtypeStruct((MATS, TRI, HALF, HALF), F32),
        compiler_params=params(),
        cost_estimate=cost(MATS * 12 * SHARE * RANK * RANK, 16 * SHARE * RANK),
    )(total)


def finish(ranks, inv, whole, rows, mine, theirs):
    for b in range(8):
        start = pl.multiple_of(ranks[b] * BLOCK, BLOCK)
        rows[b * BLOCK : (b + 1) * BLOCK] = inv[0, pl.ds(start, BLOCK), :]
    out = jnp.dot(rows[...], whole, precision=EXACT, preferred_element_type=F32)
    mine[0] = out[:HALF]
    theirs[0] = out[HALF:].astype(BF16)


def project_kernel(ranks, s, g, inv, mine, theirs, rows):
    whole = lax.dot_general(s[0], g[0], (((0,), (0,)), ((), ())), preferred_element_type=F32)
    finish(ranks, inv, whole, rows, mine, theirs)


def project(gradients, gathered, inverse, ranks):
    depth = gradients.shape[1]
    half = pl.BlockSpec((1, HALF, WIDTH), lambda n, r: (n, 0, 0))
    return pl.pallas_call(
        project_kernel,
        grid_spec=pltpu.PrefetchScalarGridSpec(
            num_scalar_prefetch=1,
            grid=(MATS,),
            in_specs=[
                pl.BlockSpec((1, depth, RANK), lambda n, r: (n, 0, 0)),
                pl.BlockSpec((1, depth, WIDTH), lambda n, r: (n, 0, 0)),
                pl.BlockSpec((1, RANK, RANK), lambda n, r: (n, 0, 0)),
            ],
            out_specs=[half, half],
            scratch_shapes=[pltpu.VMEM((RANK, RANK), F32)],
        ),
        out_shape=[
            jax.ShapeDtypeStruct((MATS, HALF, WIDTH), F32),
            jax.ShapeDtypeStruct((MATS, HALF, WIDTH), BF16),
        ],
        compiler_params=params(),
        cost_estimate=cost(MATS * 2 * RANK * WIDTH * (depth + 6 * RANK), MATS * 2 * depth * (WIDTH + RANK)),
    )(ranks, gathered, gradients, inverse)


def basis_kernel(root, s, inv, out):
    value = lax.dot_general(
        s[0], inv[0], (((1,), (1,)), ((), ())), precision=EXACT, preferred_element_type=F32
    )
    out[0] = (value * root).astype(BF16)


def make_basis(total, inverse, root):
    share = pl.BlockSpec((1, SHARE, RANK), lambda n: (n, 0, 0))
    return pl.pallas_call(
        functools.partial(basis_kernel, root),
        grid=(MATS,),
        in_specs=[share, pl.BlockSpec((1, RANK, RANK), lambda n: (n, 0, 0))],
        out_specs=share,
        out_shape=jax.ShapeDtypeStruct((MATS, SHARE, RANK), BF16),
        compiler_params=params(),
        cost_estimate=cost(4 * 12 * SHARE * RANK * RANK, 4 * SHARE * RANK * 10),
    )(total, inverse)


def inverse_kernel(where, own, other, out, gram, scaled, blocks):
    x, core = where[0], where[1]
    piece = own.shape[1]
    for j, off in enumerate(OFFS):
        start = pl.multiple_of(lax.rem(x + off, RING) * piece, piece)
        blocks[core, pl.ds(start, piece), :] = own[j]
        blocks[1 - core, pl.ds(start, piece), :] = other[j]
    for m in range(MATS):
        corner, side, last = (
            blocks[m // 2, ((m % 2) * TRI + i) * HALF : ((m % 2) * TRI + i + 1) * HALF] for i in range(TRI)
        )
        gram[m, :HALF, :HALF] = corner
        gram[m, HALF:, :HALF] = side
        gram[m, :HALF, HALF:] = jnp.transpose(side)
        gram[m, HALF:, HALF:] = last
    rows = lax.broadcasted_iota(jnp.int32, (RANK, RANK), 0)
    cols = lax.broadcasted_iota(jnp.int32, (RANK, RANK), 1)
    eye = (rows == cols).astype(F32)
    weight = jnp.where(rows > cols, 1.0, 0.5 * eye)

    def diagonal(a, axis):
        return jnp.sum(jnp.where(rows == cols, a, 0.0), axis=axis, keepdims=True)

    def halves(v):
        high = v.astype(BF16)
        return high, (v - high.astype(F32)).astype(BF16)

    def product(u, v, last=False):
        dims = (((1,), (1 if last else 0,)), ((), ()))
        return lax.dot_general(u, v, dims, preferred_element_type=F32)

    def product3(u, v, last=False):
        (a, b), (c, d) = halves(u), halves(v)
        return product(a, c, last) + (product(a, d, last) + product(b, c, last))

    def rough(value, a):
        value = value.astype(BF16)
        return product(product(value, a.astype(BF16)).astype(BF16), value, True) - eye

    def fine(value, a):
        return product3(product3(value, a), value, True) - eye

    def less(value, error):
        return value - product((weight * error).astype(BF16), value.astype(BF16))

    for m in range(MATS):
        a = gram[m]
        scaled[m] = a * lax.rsqrt(diagonal(a, 1)) * lax.rsqrt(diagonal(a, 0))
    for m in range(MATS):
        out[m] = eye - weight * (scaled[m] - eye)
    for _ in range(2):
        for m in range(MATS):
            value = out[m]
            out[m] = less(value, rough(value, scaled[m]))

    def exact_step(carry):
        count, _ = carry
        large = jnp.zeros((RANK, RANK), F32)
        for m in range(MATS):
            value = out[m]
            error = fine(value, scaled[m])
            large = jnp.maximum(large, jnp.where(error == error, jnp.abs(error), 1e9))
            large = jnp.maximum(large, jnp.where((rows == cols) & (value <= 0.0), 1e9, 0.0))
            out[m] = less(value, error)
        return count + 1, jnp.max(large)

    _, left = lax.while_loop(
        lambda c: (c[0] < NEWTON_MAX) & (c[1] > NEWTON_TOL) & (c[1] < 1e8),
        exact_step,
        (jnp.int32(0), jnp.float32(1.0)),
    )
    done = left <= NEWTON_TOL

    @pl.when(done)
    def _():
        for m in range(MATS):
            out[m] = out[m] * lax.rsqrt(diagonal(gram[m], 0))

    @pl.when(jnp.logical_not(done))
    def _():
        row_ids = lax.broadcasted_iota(jnp.int32, (RANK, 1), 0)
        col_ids = lax.broadcasted_iota(jnp.int32, (1, RANK), 1)

        def matrix(m, _):
            out[m] = eye

            def column(j, _):
                pivot_row = gram[m, pl.ds(j, 1), :]
                pivot = jnp.sum(jnp.where(col_ids == j, pivot_row, 0.0), axis=1, keepdims=True)
                values = jnp.sum(jnp.where(cols == j, gram[m], 0.0), axis=1, keepdims=True)
                factor = jnp.where(row_ids > j, values / pivot, 0.0)
                known = out[m, pl.ds(j, 1), :]
                gram[m] = gram[m] - factor * pivot_row
                out[m] = out[m] - factor * known
                out[m, pl.ds(j, 1), :] = known / jnp.sqrt(pivot)
                return 0

            return lax.fori_loop(0, RANK, column, 0)

        lax.fori_loop(0, MATS, matrix, 0)


def inverse_factors(where, own, other):
    piece = own.shape[1]
    return pl.pallas_call(
        inverse_kernel,
        grid_spec=pltpu.PrefetchScalarGridSpec(
            num_scalar_prefetch=1,
            grid=(1,),
            in_specs=[pl.BlockSpec((RING, piece, HALF), lambda n, w: (0, 0, 0))] * 2,
            out_specs=pl.BlockSpec((MATS, RANK, RANK), lambda n, w: (0, 0, 0)),
            scratch_shapes=[
                pltpu.VMEM((MATS, RANK, RANK), F32),
                pltpu.VMEM((MATS, RANK, RANK), F32),
                pltpu.VMEM((2, RING * piece, HALF), F32),
            ],
        ),
        out_shape=jax.ShapeDtypeStruct((MATS, RANK, RANK), F32),
        compiler_params=params(),
        cost_estimate=cost(8e9, 4 * MATS * RANK * RANK * 4),
    )(where, own, other)


def from_others(value, axis):
    return [shift(value, axis, -1), shift(value, axis, 1), shift(value, axis, 2)]


def x_pieces(whole):
    x = place()[0]

    def piece(off):
        return lax.dynamic_index_in_dim(whole, (x + off) % RING, 0, keepdims=False)

    def sent(off, step):
        return piece(off), "x", step

    return piece, [sent(1, 1), sent(3, -1), sent(2, 2)]


def summed_grams(grams):
    core = place()[1]
    send = lax.dynamic_slice_in_dim(grams, 2 * (1 - core), 2, 0)
    keep = lax.dynamic_slice_in_dim(grams, 2 * core, 2, 0)
    whole = (keep + shift(send, "core", 1)).reshape(RING, 2 * TRI * HALF // RING, HALF)
    piece, outgoing = x_pieces(whole)
    part = piece(0)
    for arrived in [shift(*args) for args in outgoing]:
        part = part + arrived
    for axis in ("y", "z"):
        for arrived in from_others(part, axis):
            part = part + arrived
    own = jnp.stack([part] + from_others(part, "x"))
    return own, shift(own, "core", 1)


def local(gradients, sketch):
    root = float(gradients.shape[1] * lax.axis_size("row")) ** 0.5
    grads = gradients.reshape(MATS, SHARES, SHARE, WIDTH)
    x, core, y, z = place()
    here = {"y": y, "z": z}
    pairs = (("y", "z"), ("z", "y"))

    listed, base = [], {}

    def enlist(name, rows):
        base[name] = len(listed)
        listed.extend(rows)

    links = [(sign, p) for sign in (1, -1) for p in range(2)]
    moving = {link: 2 * link[1] + (link[0] < 0) for link in links}
    enlist("far", [chunk_row(moving[link], pairs[link[1]][0], here[pairs[link[1]][0]] + 2) for link in links])
    enlist(
        "near",
        [chunk_row(moving[-s, p], pairs[p][0], here[pairs[p][0]] + s % RING) for s, p in links],
    )
    for sign in (1, -1):
        fars = [2 * p if sign == 1 else 2 * p + 1 for p in range(2)]
        enlist(("hop2", sign), [chunk_row(m, r[0], here[r[0]] + sign % RING) for m, r in zip(fars, pairs)])
    for p, (ring, _) in enumerate(pairs):
        enlist(("own", p), [chunk_row(2 * p + i, ring, here[ring]) for i in range(2)])
    table = jnp.stack([jnp.asarray(v, jnp.int32) for row in listed for v in row]).reshape(-1, 5)

    hop1, near, hop2 = {}, {}, {}
    sent = sketch_chunks(grads, sketch, table, base["far"])
    for (sign, p), value in zip(links, sent):
        hop1[p, sign] = shift(value, pairs[p][0], sign)
    table, *_ = lax.optimization_barrier((table, *sent))
    sent = sketch_chunks(grads, sketch, table, base["near"])
    for (sign, p), value in zip(links, sent):
        near[p, sign] = shift(value, pairs[p][0], sign)
    table, *_ = lax.optimization_barrier((table, *sent))
    for sign in (1, -1):
        recvs = (hop1[0, sign], hop1[1, sign])
        for p, value in enumerate(combined_chunks(grads, sketch, table, base["hop2", sign], recvs)):
            hop2[p, sign] = shift(value, pairs[p][0], sign)
    part = [
        own_and_near(grads, sketch, table, base["own", p], (near[p, -1], near[p, 1])) for p in range(2)
    ]
    held = lax.optimization_barrier((*part, *hop2.values()))
    part, hop2 = held[:2], dict(zip(hop2, held[2:]))
    owns, parts = [], []
    for p, (_, cross) in enumerate(pairs):
        own, ahead, behind, across = own_chunks(part[p], (hop2[p, 1], hop2[p, -1]))
        owns.append(own)
        parts.append([shift(ahead, cross, 1), shift(behind, cross, -1), shift(across, cross, 2)])
    total, rounded = zip(*(totals(own, arrived) for own, arrived in zip(owns, parts)))
    gathered = lax.all_gather(jnp.concatenate(rounded, axis=0), "mat", axis=1, tiled=True)
    total = jnp.concatenate(total, axis=0)

    where = jnp.stack([x, core]).astype(jnp.int32)
    inverse = inverse_factors(where, *summed_grams(gram_parts(total)))

    ranks = [(x + off) % RING * 2 + core for off in OFFS]
    ranks += [(x + off) % RING * 2 + 1 - core for off in OFFS]
    ranks = jnp.stack(ranks).astype(jnp.int32)
    basis = make_basis(total, inverse, root)
    mine, theirs = project(gradients, gathered, inverse, ranks)
    both = (mine + shift(theirs, "core", 1).astype(F32)).reshape(MATS, RING, BLOCK, WIDTH)
    out = both[:, 0]
    for j, step in ((1, 1), (2, -1), (3, 2)):
        out = out + shift(both[:, j].astype(BF16), "x", step).astype(F32)
    return basis, out


def solution(mesh):
    placed = (P(None, "row", "mat"), P("mat", None))
    return jax.shard_map(
        local,
        mesh=mesh,
        in_specs=placed,
        out_specs=(P(None, ("row", "mat"), None), P(None, "row", "mat")),
        check_vma=False,
    )
```

```python
import functools

import jax
import jax.numpy as jnp
from jax import lax
from jax.experimental import pallas as pl
from jax.experimental.pallas import tpu as pltpu
from jax.sharding import PartitionSpec as P

MATS, RANK, SHARE, WIDTH, SHARES, RING = 4, 256, 224, 512, 16, 4
HALF = RANK // 2
BLOCK = RANK // 8
OFFS = (0, 1, 3, 2)
F32, BF16 = jnp.float32, jnp.bfloat16
EXACT = lax.Precision.HIGHEST
NEWTON_TOL = 3e-4
NEWTON_MAX = 10


def params():
    return pltpu.CompilerParams(vmem_limit_bytes=52 * 1024 * 1024)


def cost(flops, moved):
    return pl.CostEstimate(flops=int(flops), bytes_accessed=int(moved), transcendentals=0)


def shift(value, axis, step):
    pairs = []
    if axis in ("y", "z"):
        for z in range(RING):
            for y in range(RING):
                to = z * RING + (y + step) % RING if axis == "y" else (z + step) % RING * RING + y
                pairs.append((z * RING + y, to))
        return lax.ppermute(value, "mat", pairs)
    for x in range(RING):
        for core in range(2):
            to = (x + step) % RING * 2 + core if axis == "x" else x * 2 + (core + step) % 2
            pairs.append((x * 2 + core, to))
    return lax.ppermute(value, "row", pairs)


def place():
    row, mat = lax.axis_index("row"), lax.axis_index("mat")
    return row // 2, row % 2, mat % RING, mat // RING


def chunk_row(index, along, dest):
    _, _, y, z = place()
    if along == "y":
        return [index] + [(z + off) % RING * RING + dest % RING for off in OFFS]
    return [index] + [dest % RING * RING + (y + off) % RING for off in OFFS]


def gradient_specs(base, step=lambda *ids: ids[0]):
    return [
        pl.BlockSpec(
            (1, 1, SHARE, WIDTH),
            lambda *a, j=j: (a[-1][base + step(*a[:-1]), 0], a[-1][base + step(*a[:-1]), 1 + j], 0, 0),
        )
        for j in range(RING)
    ]


def sketch_of(grads, sk):
    rows = jnp.concatenate([g[0, 0] for g in grads], axis=0)
    return jnp.dot(rows, sk[...], preferred_element_type=F32)


CHUNK = RING * SHARE
CHUNK_FLOPS = 2 * CHUNK * WIDTH * RANK
CHUNK_BYTES = 2 * CHUNK * (WIDTH + 2 * RANK)
CHUNK_BLOCK = (1, CHUNK, RANK)


def sketch_kernel(tab, g0, g1, g2, g3, sk, *outs):
    def run(out):
        out[0] = sketch_of((g0, g1, g2, g3), sk).astype(BF16)

    for n, out in enumerate(outs):
        pl.when(pl.program_id(0) == n)(lambda out=out: run(out))


def sketch_chunks(grads, sketch, table, base):
    return pl.pallas_call(
        sketch_kernel,
        grid_spec=pltpu.PrefetchScalarGridSpec(
            num_scalar_prefetch=1,
            grid=(4,),
            in_specs=gradient_specs(base) + [pl.BlockSpec((WIDTH, RANK), lambda n, t: (0, 0))],
            out_specs=[pl.BlockSpec(CHUNK_BLOCK, lambda n, t: (0, 0, 0))] * 4,
        ),
        out_shape=[jax.ShapeDtypeStruct((1, CHUNK, RANK), BF16)] * 4,
        compiler_params=params(),
        cost_estimate=cost(4 * CHUNK_FLOPS, 4 * CHUNK_BYTES),
    )(table, grads, grads, grads, grads, sketch)


def combine_kernel(tab, g0, g1, g2, g3, sk, *rest):
    def run(recv, out):
        term = sketch_of((g0, g1, g2, g3), sk)
        out[0] = (term + recv[0].astype(F32)).astype(BF16)

    for n, (recv, out) in enumerate(zip(rest[:MATS], rest[MATS:])):
        pl.when(pl.program_id(0) == n)(lambda recv=recv, out=out: run(recv, out))


def combined_chunks(grads, sketch, table, base, recvs):
    block = pl.BlockSpec(CHUNK_BLOCK, lambda n, t: (0, 0, 0))
    return pl.pallas_call(
        combine_kernel,
        grid_spec=pltpu.PrefetchScalarGridSpec(
            num_scalar_prefetch=1,
            grid=(MATS,),
            in_specs=gradient_specs(base)
            + [pl.BlockSpec((WIDTH, RANK), lambda n, t: (0, 0))]
            + [block] * MATS,
            out_specs=[block] * MATS,
        ),
        out_shape=[jax.ShapeDtypeStruct((1, CHUNK, RANK), BF16)] * MATS,
        compiler_params=params(),
        cost_estimate=cost(4 * CHUNK_FLOPS, 4 * CHUNK_BYTES),
    )(table, grads, grads, grads, grads, sketch, *recvs)


def near_kernel(tab, g0, g1, g2, g3, sk, *rest):
    out = rest[-1]

    def run(near):
        out[0] = sketch_of((g0, g1, g2, g3), sk) + near[0].astype(F32)

    for n, near in enumerate(rest[:-1]):
        pl.when(pl.program_id(0) == n)(lambda near=near: run(near))


def own_and_near(grads, sketch, table, base, nears):
    return pl.pallas_call(
        near_kernel,
        grid_spec=pltpu.PrefetchScalarGridSpec(
            num_scalar_prefetch=1,
            grid=(MATS,),
            in_specs=gradient_specs(base)
            + [pl.BlockSpec((WIDTH, RANK), lambda n, t: (0, 0))]
            + [pl.BlockSpec(CHUNK_BLOCK, lambda n, t: (0, 0, 0))] * MATS,
            out_specs=pl.BlockSpec(CHUNK_BLOCK, lambda n, t: (n, 0, 0)),
        ),
        out_shape=jax.ShapeDtypeStruct((MATS, CHUNK, RANK), F32),
        compiler_params=params(),
        cost_estimate=cost(4 * CHUNK_FLOPS, 4 * CHUNK_BYTES),
    )(table, grads, grads, grads, grads, sketch, *nears)


def own_kernel(part, comb0, comb1, own, ahead, behind, across):
    def run(comb):
        for j, out in enumerate((own, ahead, behind, across)):
            rows = slice(j * SHARE, (j + 1) * SHARE)
            out[0] = (part[0, rows] + comb[0, rows].astype(F32)).astype(out.dtype)

    pl.when(pl.program_id(0) == 0)(lambda: run(comb0))
    pl.when(pl.program_id(0) == 1)(lambda: run(comb1))


def own_chunks(part, pair, combs):
    share = pl.BlockSpec((1, SHARE, RANK), lambda n: (n, 0, 0))
    return pl.pallas_call(
        own_kernel,
        grid=(2,),
        in_specs=[pl.BlockSpec(CHUNK_BLOCK, lambda n: (2 * pair + n, 0, 0))]
        + [pl.BlockSpec(CHUNK_BLOCK, lambda n: (0, 0, 0))] * 2,
        out_specs=[share] * 4,
        out_shape=[jax.ShapeDtypeStruct((2, SHARE, RANK), F32)]
        + [jax.ShapeDtypeStruct((2, SHARE, RANK), BF16)] * 3,
        compiler_params=params(),
        cost_estimate=cost(2 * CHUNK * RANK, 16 * CHUNK * RANK),
    )(part, *combs)


def total_kernel(own, a, b, c, *rest):
    total, rounded = rest[-2:]
    value = own[0] + a[0].astype(F32) + b[0].astype(F32) + c[0].astype(F32)
    total[0] = value
    rounded[0] = value.astype(BF16)


def totals(pair, own, parts, done=()):
    share = pl.BlockSpec((1, SHARE, RANK), lambda n: (n, 0, 0))
    placed = pl.BlockSpec((1, SHARE, RANK), lambda n: (2 * pair + n, 0, 0))
    return pl.pallas_call(
        total_kernel,
        grid=(2,),
        in_specs=[share] * 4 + [pl.BlockSpec(memory_space=pl.ANY) for _ in done],
        out_specs=[placed, placed],
        out_shape=[
            jax.ShapeDtypeStruct((MATS, SHARE, RANK), F32),
            jax.ShapeDtypeStruct((MATS, SHARE, RANK), BF16),
        ],
        input_output_aliases={4 + i: i for i in range(len(done))},
        compiler_params=params(),
        cost_estimate=cost(2 * SHARE * RANK, 2 * SHARE * RANK * 16),
    )(own, *parts, *done)


TRI = 3


def gram_kernel(s, out):
    left = jnp.transpose(s[0])
    out[0, 0] = jnp.dot(left[:HALF], s[0, :, :HALF], precision=EXACT, preferred_element_type=F32)
    low = jnp.dot(left[HALF:], s[0], precision=EXACT, preferred_element_type=F32)
    out[0, 1] = low[:, :HALF]
    out[0, 2] = low[:, HALF:]


def gram_parts(total):
    return pl.pallas_call(
        gram_kernel,
        grid=(MATS,),
        in_specs=[pl.BlockSpec((1, SHARE, RANK), lambda n: (n, 0, 0))],
        out_specs=pl.BlockSpec((1, TRI, HALF, HALF), lambda n: (n, 0, 0, 0)),
        out_shape=jax.ShapeDtypeStruct((MATS, TRI, HALF, HALF), F32),
        compiler_params=params(),
        cost_estimate=cost(MATS * 12 * SHARE * RANK * RANK, 16 * SHARE * RANK),
    )(total)


def halves(v):
    high = v.astype(BF16)
    return high, (v - high.astype(F32)).astype(BF16)


def product(u, v, last=False):
    dims = (((1,), (1 if last else 0,)), ((), ()))
    return lax.dot_general(u, v, dims, preferred_element_type=F32)


def product3(u, v, last=False):
    (a, b), (c, d) = halves(u), halves(v)
    return product(a, c, last) + (product(a, d, last) + product(b, c, last))


PARTS = 2


def project_kernel(ranks, s_hbm, g_hbm, inv, mine, theirs, s, g, rows, s_sems, g_sems):
    depth = s.shape[1] // PARTS
    copies = {}
    for m in range(MATS):
        for k in range(PARTS):
            piece = (m, pl.ds(k * depth, depth))
            copies[m, k] = (
                pltpu.make_async_copy(s_hbm.at[piece], s.at[piece], s_sems.at[m, k]),
                pltpu.make_async_copy(g_hbm.at[piece], g.at[piece], g_sems.at[m, k]),
            )
            for copy in copies[m, k]:
                copy.start()
    for m in range(MATS):
        whole = None
        for k in range(PARTS):
            for copy in copies[m, k]:
                copy.wait()
            piece = slice(k * depth, (k + 1) * depth)
            term = lax.dot_general(
                s[m, piece], g[m, piece], (((0,), (0,)), ((), ())), preferred_element_type=F32
            )
            whole = term if whole is None else whole + term
        for b in range(8):
            start = pl.multiple_of(ranks[b] * BLOCK, BLOCK)
            rows[b * BLOCK : (b + 1) * BLOCK] = inv[m, pl.ds(start, BLOCK), :]
        out = product3(rows[...], whole)
        mine[m] = out[:HALF]
        theirs[m] = out[HALF:].astype(BF16)


def project(gradients, gathered, inverse, ranks):
    depth = gradients.shape[1]
    half = pl.BlockSpec((MATS, HALF, WIDTH), lambda n, r: (0, 0, 0))
    kept = pl.BlockSpec(memory_space=pl.ANY)
    return pl.pallas_call(
        project_kernel,
        grid_spec=pltpu.PrefetchScalarGridSpec(
            num_scalar_prefetch=1,
            grid=(1,),
            in_specs=[kept, kept, pl.BlockSpec((MATS, RANK, RANK), lambda n, r: (0, 0, 0))],
            out_specs=[half, half],
            scratch_shapes=[
                pltpu.VMEM((MATS, depth, RANK), BF16),
                pltpu.VMEM((MATS, depth, WIDTH), BF16),
                pltpu.VMEM((RANK, RANK), F32),
                pltpu.SemaphoreType.DMA((MATS, PARTS)),
                pltpu.SemaphoreType.DMA((MATS, PARTS)),
            ],
        ),
        out_shape=[
            jax.ShapeDtypeStruct((MATS, HALF, WIDTH), F32),
            jax.ShapeDtypeStruct((MATS, HALF, WIDTH), BF16),
        ],
        compiler_params=params(),
        cost_estimate=cost(MATS * 2 * RANK * WIDTH * (depth + 3 * RANK), MATS * 2 * depth * (WIDTH + RANK)),
    )(ranks, gathered, gradients, inverse)


def basis_kernel(root, s, inv, out):
    value = lax.dot_general(
        s[0], inv[0], (((1,), (1,)), ((), ())), precision=EXACT, preferred_element_type=F32
    )
    out[0] = (value * root).astype(BF16)


def make_basis(total, inverse, root):
    share = pl.BlockSpec((1, SHARE, RANK), lambda n: (n, 0, 0))
    return pl.pallas_call(
        functools.partial(basis_kernel, root),
        grid=(MATS,),
        in_specs=[share, pl.BlockSpec((1, RANK, RANK), lambda n: (n, 0, 0))],
        out_specs=share,
        out_shape=jax.ShapeDtypeStruct((MATS, SHARE, RANK), BF16),
        compiler_params=params(),
        cost_estimate=cost(4 * 12 * SHARE * RANK * RANK, 4 * SHARE * RANK * 10),
    )(total, inverse)


def inverse_kernel(where, own, other, out, gram, scaled, blocks):
    x, core = where[0], where[1]
    piece = own.shape[1]
    for j, off in enumerate(OFFS):
        start = pl.multiple_of(lax.rem(x + off, RING) * piece, piece)
        blocks[core, pl.ds(start, piece), :] = own[j]
        blocks[1 - core, pl.ds(start, piece), :] = other[j]
    for m in range(MATS):
        corner, side, last = (
            blocks[m // 2, ((m % 2) * TRI + i) * HALF : ((m % 2) * TRI + i + 1) * HALF] for i in range(TRI)
        )
        gram[m, :HALF, :HALF] = corner
        gram[m, HALF:, :HALF] = side
        gram[m, :HALF, HALF:] = jnp.transpose(side)
        gram[m, HALF:, HALF:] = last
    rows = lax.broadcasted_iota(jnp.int32, (RANK, RANK), 0)
    cols = lax.broadcasted_iota(jnp.int32, (RANK, RANK), 1)
    eye = (rows == cols).astype(F32)
    weight = jnp.where(rows > cols, 1.0, 0.5 * eye)

    def diagonal(a, axis):
        return jnp.sum(jnp.where(rows == cols, a, 0.0), axis=axis, keepdims=True)

    def rough(value, a):
        value = value.astype(BF16)
        return product(product(value, a.astype(BF16)).astype(BF16), value, True) - eye

    def fine(value, a):
        return product3(product3(value, a), value, True) - eye

    def less(value, error):
        return value - product((weight * error).astype(BF16), value.astype(BF16))

    for m in range(MATS):
        a = gram[m]
        scaled[m] = a * lax.rsqrt(diagonal(a, 1)) * lax.rsqrt(diagonal(a, 0))
    for m in range(MATS):
        out[m] = eye - weight * (scaled[m] - eye)
    for _ in range(2):
        for m in range(MATS):
            value = out[m]
            out[m] = less(value, rough(value, scaled[m]))

    def exact_step(carry):
        count, _ = carry
        large = jnp.zeros((RANK, RANK), F32)
        for m in range(MATS):
            value = out[m]
            error = fine(value, scaled[m])
            large = jnp.maximum(large, jnp.where(error == error, jnp.abs(error), 1e9))
            large = jnp.maximum(large, jnp.where((rows == cols) & (value <= 0.0), 1e9, 0.0))
            out[m] = less(value, error)
        return count + 1, jnp.max(large)

    _, left = lax.while_loop(
        lambda c: (c[0] < NEWTON_MAX) & (c[1] > NEWTON_TOL) & (c[1] < 1e8),
        exact_step,
        (jnp.int32(0), jnp.float32(1.0)),
    )
    done = left <= NEWTON_TOL

    @pl.when(done)
    def _():
        for m in range(MATS):
            out[m] = out[m] * lax.rsqrt(diagonal(gram[m], 0))

    @pl.when(jnp.logical_not(done))
    def _():
        row_ids = lax.broadcasted_iota(jnp.int32, (RANK, 1), 0)
        col_ids = lax.broadcasted_iota(jnp.int32, (1, RANK), 1)

        def matrix(m, _):
            out[m] = eye

            def column(j, _):
                pivot_row = gram[m, pl.ds(j, 1), :]
                pivot = jnp.sum(jnp.where(col_ids == j, pivot_row, 0.0), axis=1, keepdims=True)
                values = jnp.sum(jnp.where(cols == j, gram[m], 0.0), axis=1, keepdims=True)
                factor = jnp.where(row_ids > j, values / pivot, 0.0)
                known = out[m, pl.ds(j, 1), :]
                gram[m] = gram[m] - factor * pivot_row
                out[m] = out[m] - factor * known
                out[m, pl.ds(j, 1), :] = known / jnp.sqrt(pivot)
                return 0

            return lax.fori_loop(0, RANK, column, 0)

        lax.fori_loop(0, MATS, matrix, 0)


def inverse_factors(where, own, other):
    piece = own.shape[1]
    return pl.pallas_call(
        inverse_kernel,
        grid_spec=pltpu.PrefetchScalarGridSpec(
            num_scalar_prefetch=1,
            grid=(1,),
            in_specs=[pl.BlockSpec((RING, piece, HALF), lambda n, w: (0, 0, 0))] * 2,
            out_specs=pl.BlockSpec((MATS, RANK, RANK), lambda n, w: (0, 0, 0)),
            scratch_shapes=[
                pltpu.VMEM((MATS, RANK, RANK), F32),
                pltpu.VMEM((MATS, RANK, RANK), F32),
                pltpu.VMEM((2, RING * piece, HALF), F32),
            ],
        ),
        out_shape=jax.ShapeDtypeStruct((MATS, RANK, RANK), F32),
        compiler_params=params(),
        cost_estimate=cost(8e9, 4 * MATS * RANK * RANK * 4),
    )(where, own, other)


def from_others(value, axis):
    return [shift(value, axis, -1), shift(value, axis, 1), shift(value, axis, 2)]


def x_pieces(whole):
    x = place()[0]

    def piece(off):
        return lax.dynamic_index_in_dim(whole, (x + off) % RING, 0, keepdims=False)

    def sent(off, step):
        return piece(off), "x", step

    return piece, [sent(1, 1), sent(3, -1), sent(2, 2)]


def summed_grams(grams):
    core = place()[1]
    send = lax.dynamic_slice_in_dim(grams, 2 * (1 - core), 2, 0)
    keep = lax.dynamic_slice_in_dim(grams, 2 * core, 2, 0)
    whole = (keep + shift(send, "core", 1)).reshape(RING, 2 * TRI * HALF // RING, HALF)
    piece, outgoing = x_pieces(whole)
    part = piece(0)
    for arrived in [shift(*args) for args in outgoing]:
        part = part + arrived
    for axis in ("y", "z"):
        for arrived in from_others(part, axis):
            part = part + arrived
    own = jnp.stack([part] + from_others(part, "x"))
    return own, shift(own, "core", 1)


def local(gradients, sketch):
    root = float(gradients.shape[1] * lax.axis_size("row")) ** 0.5
    grads = gradients.reshape(MATS, SHARES, SHARE, WIDTH)
    x, core, y, z = place()
    here = {"y": y, "z": z}
    pairs = (("y", "z"), ("z", "y"))

    listed, base = [], {}

    def enlist(name, rows):
        base[name] = len(listed)
        listed.extend(rows)

    links = [(sign, p) for sign in (1, -1) for p in range(2)]
    moving = {link: 2 * link[1] + (link[0] < 0) for link in links}
    enlist("far", [chunk_row(moving[link], pairs[link[1]][0], here[pairs[link[1]][0]] + 2) for link in links])
    enlist(
        "near",
        [chunk_row(moving[-s, p], pairs[p][0], here[pairs[p][0]] + s % RING) for s, p in links],
    )
    for sign in (1, -1):
        fars = [2 * p if sign == 1 else 2 * p + 1 for p in range(2)]
        enlist(("hop2", sign), [chunk_row(m, r[0], here[r[0]] + sign % RING) for m, r in zip(fars, pairs)])
    for p, (ring, _) in enumerate(pairs):
        enlist(("own", p), [chunk_row(2 * p + i, ring, here[ring]) for i in range(2)])
    table = jnp.stack([jnp.asarray(v, jnp.int32) for row in listed for v in row]).reshape(-1, 5)

    hop1, near, hop2 = {}, {}, {}
    sent = sketch_chunks(grads, sketch, table, base["far"])
    for (sign, p), value in zip(links, sent):
        hop1[p, sign] = shift(value, pairs[p][0], sign)
    table, *_ = lax.optimization_barrier((table, *sent))
    sent = sketch_chunks(grads, sketch, table, base["near"])
    for (sign, p), value in zip(links, sent):
        near[p, sign] = shift(value, pairs[p][0], sign)
    table, *_ = lax.optimization_barrier((table, *sent))
    recvs = [hop1[p, sign] for sign, p in links]
    for (sign, p), value in zip(links, combined_chunks(grads, sketch, table, base["hop2", 1], recvs)):
        hop2[p, sign] = shift(value, pairs[p][0], sign)
    nears = (near[0, -1], near[0, 1], near[1, -1], near[1, 1])
    part = own_and_near(grads, sketch, table, base["own", 0], nears)
    held = lax.optimization_barrier((part, *hop2.values()))
    part, hop2 = held[0], dict(zip(hop2, held[1:]))
    owns, parts = [], []
    for p, (_, cross) in enumerate(pairs):
        own, ahead, behind, across = own_chunks(part, p, (hop2[p, 1], hop2[p, -1]))
        owns.append(own)
        parts.append([shift(ahead, cross, 1), shift(behind, cross, -1), shift(across, cross, 2)])
    done = totals(0, owns[0], parts[0])
    total, rounded = totals(1, owns[1], parts[1], done)
    gathered = lax.all_gather(rounded, "mat", axis=1, tiled=True)

    where = jnp.stack([x, core]).astype(jnp.int32)
    inverse = inverse_factors(where, *summed_grams(gram_parts(total)))

    ranks = [(x + off) % RING * 2 + core for off in OFFS]
    ranks += [(x + off) % RING * 2 + 1 - core for off in OFFS]
    ranks = jnp.stack(ranks).astype(jnp.int32)
    basis = make_basis(total, inverse, root)
    mine, theirs = project(gradients, gathered, inverse, ranks)
    both = (mine + shift(theirs, "core", 1).astype(F32)).reshape(MATS, RING, BLOCK, WIDTH)
    out = both[:, 0]
    for j, step in ((1, 1), (2, -1), (3, 2)):
        out = out + shift(both[:, j].astype(BF16), "x", step).astype(F32)
    return basis, out


def solution(mesh):
    placed = (P(None, "row", "mat"), P("mat", None))
    return jax.shard_map(
        local,
        mesh=mesh,
        in_specs=placed,
        out_specs=(P(None, ("row", "mat"), None), P(None, "row", "mat")),
        check_vma=False,
    )
```

```python
import functools

import jax
import jax.numpy as jnp
from jax import lax
from jax.experimental import pallas as pl
from jax.experimental.pallas import tpu as pltpu
from jax.sharding import PartitionSpec as P

MATS, RANK, SHARE, WIDTH, SHARES, RING = 4, 256, 224, 512, 16, 4
HALF = RANK // 2
BLOCK = RANK // 8
OFFS = (0, 1, 3, 2)
F32, BF16 = jnp.float32, jnp.bfloat16
EXACT = lax.Precision.HIGHEST
NEWTON_TOL = 3e-4
NEWTON_MAX = 10


def params():
    return pltpu.CompilerParams(vmem_limit_bytes=52 * 1024 * 1024)


def cost(flops, moved):
    return pl.CostEstimate(flops=int(flops), bytes_accessed=int(moved), transcendentals=0)


def shift(value, axis, step):
    pairs = []
    if axis in ("y", "z"):
        for z in range(RING):
            for y in range(RING):
                to = z * RING + (y + step) % RING if axis == "y" else (z + step) % RING * RING + y
                pairs.append((z * RING + y, to))
        return lax.ppermute(value, "mat", pairs)
    for x in range(RING):
        for core in range(2):
            to = (x + step) % RING * 2 + core if axis == "x" else x * 2 + (core + step) % 2
            pairs.append((x * 2 + core, to))
    return lax.ppermute(value, "row", pairs)


def place():
    row, mat = lax.axis_index("row"), lax.axis_index("mat")
    return row // 2, row % 2, mat % RING, mat // RING


def chunk_row(index, along, dest):
    _, _, y, z = place()
    if along == "y":
        return [index] + [(z + off) % RING * RING + dest % RING for off in OFFS]
    return [index] + [dest % RING * RING + (y + off) % RING for off in OFFS]


def gradient_specs(base, step=lambda *ids: ids[0]):
    return [
        pl.BlockSpec(
            (1, 1, SHARE, WIDTH),
            lambda *a, j=j: (a[-1][base + step(*a[:-1]), 0], a[-1][base + step(*a[:-1]), 1 + j], 0, 0),
        )
        for j in range(RING)
    ]


def sketch_of(grads, sk):
    rows = jnp.concatenate([g[0, 0] for g in grads], axis=0)
    return jnp.dot(rows, sk[...], preferred_element_type=F32)


CHUNK = RING * SHARE
CHUNK_FLOPS = 2 * CHUNK * WIDTH * RANK
CHUNK_BYTES = 2 * CHUNK * (WIDTH + 2 * RANK)
CHUNK_BLOCK = (1, CHUNK, RANK)


def sketch_kernel(tab, g0, g1, g2, g3, sk, *outs):
    def run(out):
        out[0] = sketch_of((g0, g1, g2, g3), sk).astype(BF16)

    for n, out in enumerate(outs):
        pl.when(pl.program_id(0) == n)(lambda out=out: run(out))


def sketch_chunks(grads, sketch, table, base):
    return pl.pallas_call(
        sketch_kernel,
        grid_spec=pltpu.PrefetchScalarGridSpec(
            num_scalar_prefetch=1,
            grid=(4,),
            in_specs=gradient_specs(base) + [pl.BlockSpec((WIDTH, RANK), lambda n, t: (0, 0))],
            out_specs=[pl.BlockSpec(CHUNK_BLOCK, lambda n, t: (0, 0, 0))] * 4,
        ),
        out_shape=[jax.ShapeDtypeStruct((1, CHUNK, RANK), BF16)] * 4,
        compiler_params=params(),
        cost_estimate=cost(4 * CHUNK_FLOPS, 4 * CHUNK_BYTES),
    )(table, grads, grads, grads, grads, sketch)


def combine_kernel(tab, g0, g1, g2, g3, sk, *rest):
    def run(recv, out):
        term = sketch_of((g0, g1, g2, g3), sk)
        out[0] = (term + recv[0].astype(F32)).astype(BF16)

    for n, (recv, out) in enumerate(zip(rest[:MATS], rest[MATS:])):
        pl.when(pl.program_id(0) == n)(lambda recv=recv, out=out: run(recv, out))


def combined_chunks(grads, sketch, table, base, recvs):
    block = pl.BlockSpec(CHUNK_BLOCK, lambda n, t: (0, 0, 0))
    return pl.pallas_call(
        combine_kernel,
        grid_spec=pltpu.PrefetchScalarGridSpec(
            num_scalar_prefetch=1,
            grid=(MATS,),
            in_specs=gradient_specs(base)
            + [pl.BlockSpec((WIDTH, RANK), lambda n, t: (0, 0))]
            + [block] * MATS,
            out_specs=[block] * MATS,
        ),
        out_shape=[jax.ShapeDtypeStruct((1, CHUNK, RANK), BF16)] * MATS,
        compiler_params=params(),
        cost_estimate=cost(4 * CHUNK_FLOPS, 4 * CHUNK_BYTES),
    )(table, grads, grads, grads, grads, sketch, *recvs)


def near_kernel(tab, g0, g1, g2, g3, sk, *rest):
    out = rest[-1]

    def run(near):
        out[0] = sketch_of((g0, g1, g2, g3), sk) + near[0].astype(F32)

    for n, near in enumerate(rest[:-1]):
        pl.when(pl.program_id(0) == n)(lambda near=near: run(near))


def own_and_near(grads, sketch, table, base, nears):
    return pl.pallas_call(
        near_kernel,
        grid_spec=pltpu.PrefetchScalarGridSpec(
            num_scalar_prefetch=1,
            grid=(MATS,),
            in_specs=gradient_specs(base)
            + [pl.BlockSpec((WIDTH, RANK), lambda n, t: (0, 0))]
            + [pl.BlockSpec(CHUNK_BLOCK, lambda n, t: (0, 0, 0))] * MATS,
            out_specs=pl.BlockSpec(CHUNK_BLOCK, lambda n, t: (n, 0, 0)),
        ),
        out_shape=jax.ShapeDtypeStruct((MATS, CHUNK, RANK), F32),
        compiler_params=params(),
        cost_estimate=cost(4 * CHUNK_FLOPS, 4 * CHUNK_BYTES),
    )(table, grads, grads, grads, grads, sketch, *nears)


def own_kernel(part, comb0, comb1, own, ahead, behind, across):
    def run(comb):
        for j, out in enumerate((own, ahead, behind, across)):
            rows = slice(j * SHARE, (j + 1) * SHARE)
            out[0] = (part[0, rows] + comb[0, rows].astype(F32)).astype(out.dtype)

    pl.when(pl.program_id(0) == 0)(lambda: run(comb0))
    pl.when(pl.program_id(0) == 1)(lambda: run(comb1))


def own_chunks(part, pair, combs):
    share = pl.BlockSpec((1, SHARE, RANK), lambda n: (n, 0, 0))
    return pl.pallas_call(
        own_kernel,
        grid=(2,),
        in_specs=[pl.BlockSpec(CHUNK_BLOCK, lambda n: (2 * pair + n, 0, 0))]
        + [pl.BlockSpec(CHUNK_BLOCK, lambda n: (0, 0, 0))] * 2,
        out_specs=[share] * 4,
        out_shape=[jax.ShapeDtypeStruct((2, SHARE, RANK), F32)]
        + [jax.ShapeDtypeStruct((2, SHARE, RANK), BF16)] * 3,
        compiler_params=params(),
        cost_estimate=cost(2 * CHUNK * RANK, 16 * CHUNK * RANK),
    )(part, *combs)


def total_kernel(own, a, b, c, *rest):
    total, rounded = rest[-2:]
    value = own[0] + a[0].astype(F32) + b[0].astype(F32) + c[0].astype(F32)
    total[0] = value
    rounded[0] = value.astype(BF16)


def totals(pair, own, parts, done=()):
    share = pl.BlockSpec((1, SHARE, RANK), lambda n: (n, 0, 0))
    placed = pl.BlockSpec((1, SHARE, RANK), lambda n: (2 * pair + n, 0, 0))
    return pl.pallas_call(
        total_kernel,
        grid=(2,),
        in_specs=[share] * 4 + [pl.BlockSpec(memory_space=pl.ANY) for _ in done],
        out_specs=[placed, placed],
        out_shape=[
            jax.ShapeDtypeStruct((MATS, SHARE, RANK), F32),
            jax.ShapeDtypeStruct((MATS, SHARE, RANK), BF16),
        ],
        input_output_aliases={4 + i: i for i in range(len(done))},
        compiler_params=params(),
        cost_estimate=cost(2 * SHARE * RANK, 2 * SHARE * RANK * 16),
    )(own, *parts, *done)


TRI = 3


def gram_kernel(s, out):
    left = jnp.transpose(s[0])
    out[0, 0] = jnp.dot(left[:HALF], s[0, :, :HALF], precision=EXACT, preferred_element_type=F32)
    low = jnp.dot(left[HALF:], s[0], precision=EXACT, preferred_element_type=F32)
    out[0, 1] = low[:, :HALF]
    out[0, 2] = low[:, HALF:]


def gram_parts(total):
    return pl.pallas_call(
        gram_kernel,
        grid=(MATS,),
        in_specs=[pl.BlockSpec((1, SHARE, RANK), lambda n: (n, 0, 0))],
        out_specs=pl.BlockSpec((1, TRI, HALF, HALF), lambda n: (n, 0, 0, 0)),
        out_shape=jax.ShapeDtypeStruct((MATS, TRI, HALF, HALF), F32),
        compiler_params=params(),
        cost_estimate=cost(MATS * 12 * SHARE * RANK * RANK, 16 * SHARE * RANK),
    )(total)


def halves(v):
    high = v.astype(BF16)
    return high, (v - high.astype(F32)).astype(BF16)


def product(u, v, last=False):
    dims = (((1,), (1 if last else 0,)), ((), ()))
    return lax.dot_general(u, v, dims, preferred_element_type=F32)


def product3(u, v, last=False):
    (a, b), (c, d) = halves(u), halves(v)
    return product(a, c, last) + (product(a, d, last) + product(b, c, last))


PARTS = 2


def project_kernel(ranks, s_hbm, g_hbm, inv, mine, theirs, s, g, rows, s_sems, g_sems):
    depth = s.shape[1] // PARTS
    copies = {}
    for m in range(MATS):
        for k in range(PARTS):
            piece = (m, pl.ds(k * depth, depth))
            copies[m, k] = (
                pltpu.make_async_copy(s_hbm.at[piece], s.at[piece], s_sems.at[m, k]),
                pltpu.make_async_copy(g_hbm.at[piece], g.at[piece], g_sems.at[m, k]),
            )
            for copy in copies[m, k]:
                copy.start()
    for m in range(MATS):
        whole = None
        for k in range(PARTS):
            for copy in copies[m, k]:
                copy.wait()
            piece = slice(k * depth, (k + 1) * depth)
            term = lax.dot_general(
                s[m, piece], g[m, piece], (((0,), (0,)), ((), ())), preferred_element_type=F32
            )
            whole = term if whole is None else whole + term
        for b in range(8):
            start = pl.multiple_of(ranks[b] * BLOCK, BLOCK)
            rows[b * BLOCK : (b + 1) * BLOCK] = inv[m, pl.ds(start, BLOCK), :]
        out = product3(rows[...], whole)
        mine[m] = out[:HALF]
        theirs[m] = out[HALF:].astype(BF16)


def project(gradients, gathered, inverse, ranks):
    depth = gradients.shape[1]
    half = pl.BlockSpec((MATS, HALF, WIDTH), lambda n, r: (0, 0, 0))
    kept = pl.BlockSpec(memory_space=pl.ANY)
    return pl.pallas_call(
        project_kernel,
        grid_spec=pltpu.PrefetchScalarGridSpec(
            num_scalar_prefetch=1,
            grid=(1,),
            in_specs=[kept, kept, pl.BlockSpec((MATS, RANK, RANK), lambda n, r: (0, 0, 0))],
            out_specs=[half, half],
            scratch_shapes=[
                pltpu.VMEM((MATS, depth, RANK), BF16),
                pltpu.VMEM((MATS, depth, WIDTH), BF16),
                pltpu.VMEM((RANK, RANK), F32),
                pltpu.SemaphoreType.DMA((MATS, PARTS)),
                pltpu.SemaphoreType.DMA((MATS, PARTS)),
            ],
        ),
        out_shape=[
            jax.ShapeDtypeStruct((MATS, HALF, WIDTH), F32),
            jax.ShapeDtypeStruct((MATS, HALF, WIDTH), BF16),
        ],
        compiler_params=params(),
        cost_estimate=cost(MATS * 2 * RANK * WIDTH * (depth + 3 * RANK), MATS * 2 * depth * (WIDTH + RANK)),
    )(ranks, gathered, gradients, inverse)


def basis_kernel(root, s, inv, out):
    value = lax.dot_general(
        s[0], inv[0], (((1,), (1,)), ((), ())), precision=EXACT, preferred_element_type=F32
    )
    out[0] = (value * root).astype(BF16)


def make_basis(total, inverse, root):
    share = pl.BlockSpec((1, SHARE, RANK), lambda n: (n, 0, 0))
    return pl.pallas_call(
        functools.partial(basis_kernel, root),
        grid=(MATS,),
        in_specs=[share, pl.BlockSpec((1, RANK, RANK), lambda n: (n, 0, 0))],
        out_specs=share,
        out_shape=jax.ShapeDtypeStruct((MATS, SHARE, RANK), BF16),
        compiler_params=params(),
        cost_estimate=cost(4 * 12 * SHARE * RANK * RANK, 4 * SHARE * RANK * 10),
    )(total, inverse)


def inverse_kernel(where, own, other, out, gram, scaled, blocks):
    x, core = where[0], where[1]
    piece = own.shape[1]
    for j, off in enumerate(OFFS):
        start = pl.multiple_of(lax.rem(x + off, RING) * piece, piece)
        blocks[core, pl.ds(start, piece), :] = own[j]
        blocks[1 - core, pl.ds(start, piece), :] = other[j]
    for m in range(MATS):
        corner, side, last = (
            blocks[m // 2, ((m % 2) * TRI + i) * HALF : ((m % 2) * TRI + i + 1) * HALF] for i in range(TRI)
        )
        gram[m, :HALF, :HALF] = corner
        gram[m, HALF:, :HALF] = side
        gram[m, :HALF, HALF:] = jnp.transpose(side)
        gram[m, HALF:, HALF:] = last
    rows = lax.broadcasted_iota(jnp.int32, (RANK, RANK), 0)
    cols = lax.broadcasted_iota(jnp.int32, (RANK, RANK), 1)
    eye = (rows == cols).astype(F32)
    weight = jnp.where(rows > cols, 1.0, 0.5 * eye)

    def diagonal(a, axis):
        return jnp.sum(jnp.where(rows == cols, a, 0.0), axis=axis, keepdims=True)

    def rough(value, a):
        value = value.astype(BF16)
        return product(product(value, a.astype(BF16)).astype(BF16), value, True) - eye

    def fine(value, a):
        return product3(product3(value, a), value, True) - eye

    def less(value, error):
        return value - product((weight * error).astype(BF16), value.astype(BF16))

    for m in range(MATS):
        a = gram[m]
        scaled[m] = a * lax.rsqrt(diagonal(a, 1)) * lax.rsqrt(diagonal(a, 0))
    for m in range(MATS):
        out[m] = eye - weight * (scaled[m] - eye)
    for _ in range(2):
        for m in range(MATS):
            value = out[m]
            out[m] = less(value, rough(value, scaled[m]))

    def exact_step(carry):
        count, _ = carry
        large = jnp.zeros((RANK, RANK), F32)
        for m in range(MATS):
            value = out[m]
            error = fine(value, scaled[m])
            large = jnp.maximum(large, jnp.where(error == error, jnp.abs(error), 1e9))
            large = jnp.maximum(large, jnp.where((rows == cols) & (value <= 0.0), 1e9, 0.0))
            out[m] = less(value, error)
        return count + 1, jnp.max(large)

    _, left = lax.while_loop(
        lambda c: (c[0] < NEWTON_MAX) & (c[1] > NEWTON_TOL) & (c[1] < 1e8),
        exact_step,
        (jnp.int32(0), jnp.float32(1.0)),
    )
    done = left <= NEWTON_TOL

    @pl.when(done)
    def _():
        for m in range(MATS):
            out[m] = out[m] * lax.rsqrt(diagonal(gram[m], 0))

    @pl.when(jnp.logical_not(done))
    def _():
        row_ids = lax.broadcasted_iota(jnp.int32, (RANK, 1), 0)
        col_ids = lax.broadcasted_iota(jnp.int32, (1, RANK), 1)

        def matrix(m, _):
            out[m] = eye

            def column(j, _):
                pivot_row = gram[m, pl.ds(j, 1), :]
                pivot = jnp.sum(jnp.where(col_ids == j, pivot_row, 0.0), axis=1, keepdims=True)
                values = jnp.sum(jnp.where(cols == j, gram[m], 0.0), axis=1, keepdims=True)
                factor = jnp.where(row_ids > j, values / pivot, 0.0)
                known = out[m, pl.ds(j, 1), :]
                gram[m] = gram[m] - factor * pivot_row
                out[m] = out[m] - factor * known
                out[m, pl.ds(j, 1), :] = known / jnp.sqrt(pivot)
                return 0

            return lax.fori_loop(0, RANK, column, 0)

        lax.fori_loop(0, MATS, matrix, 0)


def inverse_factors(where, own, other):
    piece = own.shape[1]
    return pl.pallas_call(
        inverse_kernel,
        grid_spec=pltpu.PrefetchScalarGridSpec(
            num_scalar_prefetch=1,
            grid=(1,),
            in_specs=[pl.BlockSpec((RING, piece, HALF), lambda n, w: (0, 0, 0))] * 2,
            out_specs=pl.BlockSpec((MATS, RANK, RANK), lambda n, w: (0, 0, 0)),
            scratch_shapes=[
                pltpu.VMEM((MATS, RANK, RANK), F32),
                pltpu.VMEM((MATS, RANK, RANK), F32),
                pltpu.VMEM((2, RING * piece, HALF), F32),
            ],
        ),
        out_shape=jax.ShapeDtypeStruct((MATS, RANK, RANK), F32),
        compiler_params=params(),
        cost_estimate=cost(8e9, 4 * MATS * RANK * RANK * 4),
    )(where, own, other)


def from_others(value, axis):
    return [shift(value, axis, -1), shift(value, axis, 1), shift(value, axis, 2)]


def quarter(whole, axis):
    here = dict(zip(("x", "core", "y", "z"), place()))[axis]

    def piece(off):
        return lax.dynamic_index_in_dim(whole, (here + off) % RING, 0, keepdims=False)

    part = piece(0)
    for off, step in ((1, 1), (3, -1), (2, 2)):
        part = part + shift(piece(off), axis, step)
    return part


def summed_grams(grams):
    _, core, y, _ = place()
    send = lax.dynamic_slice_in_dim(grams, 2 * (1 - core), 2, 0)
    keep = lax.dynamic_slice_in_dim(grams, 2 * core, 2, 0)
    whole = (keep + shift(send, "core", 1)).reshape(RING, 2 * TRI * HALF // RING, HALF)
    part = quarter(whole, "x")
    small = quarter(part.reshape(RING, part.shape[0] // RING, HALF), "y")
    for arrived in from_others(small, "z"):
        small = small + arrived
    after, before, opposite = from_others(small, "y")
    part = jnp.roll(jnp.stack([small, after, opposite, before]), y, axis=0).reshape(part.shape)
    own = jnp.stack([part] + from_others(part, "x"))
    return own, shift(own, "core", 1)


def local(gradients, sketch):
    root = float(gradients.shape[1] * lax.axis_size("row")) ** 0.5
    grads = gradients.reshape(MATS, SHARES, SHARE, WIDTH)
    x, core, y, z = place()
    here = {"y": y, "z": z}
    pairs = (("y", "z"), ("z", "y"))

    listed, base = [], {}

    def enlist(name, rows):
        base[name] = len(listed)
        listed.extend(rows)

    links = [(sign, p) for sign in (1, -1) for p in range(2)]
    moving = {link: 2 * link[1] + (link[0] < 0) for link in links}
    enlist("far", [chunk_row(moving[link], pairs[link[1]][0], here[pairs[link[1]][0]] + 2) for link in links])
    enlist(
        "near",
        [chunk_row(moving[-s, p], pairs[p][0], here[pairs[p][0]] + s % RING) for s, p in links],
    )
    for sign in (1, -1):
        fars = [2 * p if sign == 1 else 2 * p + 1 for p in range(2)]
        enlist(("hop2", sign), [chunk_row(m, r[0], here[r[0]] + sign % RING) for m, r in zip(fars, pairs)])
    for p, (ring, _) in enumerate(pairs):
        enlist(("own", p), [chunk_row(2 * p + i, ring, here[ring]) for i in range(2)])
    table = jnp.stack([jnp.asarray(v, jnp.int32) for row in listed for v in row]).reshape(-1, 5)

    hop1, near, hop2 = {}, {}, {}
    sent = sketch_chunks(grads, sketch, table, base["far"])
    for (sign, p), value in zip(links, sent):
        hop1[p, sign] = shift(value, pairs[p][0], sign)
    table, *_ = lax.optimization_barrier((table, *sent))
    sent = sketch_chunks(grads, sketch, table, base["near"])
    for (sign, p), value in zip(links, sent):
        near[p, sign] = shift(value, pairs[p][0], sign)
    table, *_ = lax.optimization_barrier((table, *sent))
    recvs = [hop1[p, sign] for sign, p in links]
    for (sign, p), value in zip(links, combined_chunks(grads, sketch, table, base["hop2", 1], recvs)):
        hop2[p, sign] = shift(value, pairs[p][0], sign)
    nears = (near[0, -1], near[0, 1], near[1, -1], near[1, 1])
    part = own_and_near(grads, sketch, table, base["own", 0], nears)
    held = lax.optimization_barrier((part, *hop2.values()))
    part, hop2 = held[0], dict(zip(hop2, held[1:]))
    owns, parts = [], []
    for p, (_, cross) in enumerate(pairs):
        own, ahead, behind, across = own_chunks(part, p, (hop2[p, 1], hop2[p, -1]))
        owns.append(own)
        parts.append([shift(ahead, cross, 1), shift(behind, cross, -1), shift(across, cross, 2)])
    done = totals(0, owns[0], parts[0])
    total, rounded = totals(1, owns[1], parts[1], done)
    gathered = lax.all_gather(rounded, "mat", axis=1, tiled=True)

    where = jnp.stack([x, core]).astype(jnp.int32)
    inverse = inverse_factors(where, *summed_grams(gram_parts(total)))

    ranks = [(x + off) % RING * 2 + core for off in OFFS]
    ranks += [(x + off) % RING * 2 + 1 - core for off in OFFS]
    ranks = jnp.stack(ranks).astype(jnp.int32)
    basis = make_basis(total, inverse, root)
    mine, theirs = project(gradients, gathered, inverse, ranks)
    both = (mine + shift(theirs, "core", 1).astype(F32)).reshape(MATS, RING, BLOCK, WIDTH)
    out = both[:, 0]
    for j, step in ((1, 1), (2, -1), (3, 2)):
        out = out + shift(both[:, j].astype(BF16), "x", step).astype(F32)
    return basis, out


def solution(mesh):
    placed = (P(None, "row", "mat"), P("mat", None))
    return jax.shard_map(
        local,
        mesh=mesh,
        in_specs=placed,
        out_specs=(P(None, ("row", "mat"), None), P(None, "row", "mat")),
        check_vma=False,
    )
```
